768 devices in a mesh: rep: 96 (over x, z, core), leaf: 8 (over y).
Axes of the slice: x: 4, y: 8, z: 12, core: 2. Of those that a mesh axis runs over, the one named last changes fastest.
Arguments:
- grads: bfloat16 [96, 8, 64, 24576], P('rep', 'leaf'), may hold values from -6 to 6
- momentum: float32 [96, 64, 24576], P('rep', None, 'leaf'), may hold values from -6 to 6
- picks: int32 [96, 1, 384, 32], P('rep', None, 'leaf'), may hold values from 0 to 4095, as said below
- counts: int32 [96, 1, 384], P('rep', None, 'leaf'), may hold values from 1 to 32, as said below
Outputs:
- new_momentum: float32 [96, 64, 24576], P('rep', None, 'leaf')
- update: bfloat16 [64, 24576], replicated
The draws below stay inside these ranges and needn't reach their ends.
Inputs may be any that keep to these rules, and one draw needn't show every extreme that they name: `picks`: within one block of one replica the 32 indices are distinct, padding slots included. `counts`: every replica has a block with all 32 slots used.
All inputs are finite; a program needn't handle non-finite values.
Results may differ from the reference program's by a relative error of at most 0.02.
Values may be sent and summed in bfloat16 or wider, within the bound.
No kernel may reach another device: no remote copies, remote signals or barrier semaphores. Data moves between devices by JAX's collectives and lax.ppermute only.
A program may use at most 64 MiB of HBM per device.

```python
import jax
import jax.numpy as jnp
from jax import lax

FF = 24576
ROWS = 64
SPAN = 64
K_MAX = 32
RB = 1
CC = 384
N_REP = 96
N_LEAF = 8


def draw_picks(key, part):
    key = jax.random.fold_in(key, 11)
    shape_one = (ROWS // SPAN, FF // SPAN, SPAN * SPAN)

    def one_replica(rep_key):
        scores = jax.random.randint(rep_key, shape_one, 0, 2 ** 18) * (SPAN * SPAN)
        scores = scores + lax.broadcasted_iota(jnp.int32, shape_one, 2)
        ordering = jnp.argsort(scores, axis=-1)
        return ordering[..., :K_MAX].astype(jnp.int32)
    rep_keys = jax.random.split(key, N_REP)
    return lax.map(one_replica, rep_keys)


def draw_counts(key, part):
    key = jax.random.fold_in(key, 23)
    first_key, second_key, third_key = jax.random.split(key, 3)
    blocks_all = ROWS // SPAN * (FF // SPAN)
    first = jax.random.randint(first_key, (N_REP, blocks_all), 1, K_MAX + 1)
    second = jax.random.randint(second_key, (N_REP, blocks_all), 1, K_MAX + 1)
    lower = jnp.minimum(first, second)
    position = jax.random.randint(third_key, (N_REP, 1), 0, blocks_all)
    column_ids = lax.broadcasted_iota(jnp.int32, (N_REP, blocks_all), 1)
    filled = jnp.where(column_ids == position, K_MAX, lower).astype(jnp.int32)
    return filled.reshape(N_REP, ROWS // SPAN, FF // SPAN)


def block_levels(rng, extent, cuts, smallest, high):
    factor_of, own = 1.0, jax.random.fold_in(rng, 6)
    for dim, parts in cuts:
        heights = jnp.exp(jax.random.uniform(jax.random.fold_in(own, dim), (parts,), jnp.float32, smallest / len(cuts), high / len(cuts)))
        factor_of = factor_of * jnp.repeat(heights, extent[dim] // parts).reshape([-1 if axis == dim else 1 for axis in range(len(extent))])
    return factor_of


def noise(stream_key, dims, scale, bound, cuts=(), dtype=jnp.bfloat16):
    factor_of = block_levels(stream_key, dims, cuts, -0.22, 0.18) if cuts else 1.0
    entries = jax.random.normal(stream_key, dims, jnp.float32) * scale * factor_of
    return jnp.minimum(jnp.maximum(entries, -bound), bound).astype(dtype)


def setup_inputs(seed: int = 0) -> dict:
    seeds = jax.random.split(jax.random.key(seed), 5)
    return {
        "grads": noise(seeds[0], (N_REP, N_LEAF, ROWS, FF), 1.0, 6.0, ((0, 96), (1, 8))),
        "momentum": noise(seeds[1], (N_REP, ROWS, FF), 1.0, 6.0, ((0, 96), (2, 8)), jnp.float32),
        "picks": draw_picks(jax.random.fold_in(seeds[4], 71), 0),
        "counts": draw_counts(jax.random.fold_in(seeds[4], 71), 0),
    }


def dct_table(width):
    freq_rows = lax.broadcasted_iota(jnp.float32, (width, width), 0)
    cell_cols = lax.broadcasted_iota(jnp.float32, (width, width), 1)
    scaling = jnp.where(freq_rows == 0.0, jnp.sqrt(1.0 / width), jnp.sqrt(2.0 / width)).astype(jnp.float32)
    return (scaling * jnp.cos(jnp.pi * (2.0 * cell_cols + 1.0) * freq_rows / (2.0 * width))).astype(jnp.float32)

def forward(field, cosines):
    width = cosines.shape[0]
    blocks = field.reshape(field.shape[0] // width, width, field.shape[1] // width, width)
    halfway = jnp.einsum('ui,bicj->bucj', cosines, blocks, precision=lax.Precision.HIGHEST)
    coeffs = jnp.einsum('bucj,vj->bcuv', halfway, cosines, precision=lax.Precision.HIGHEST)
    return coeffs.reshape(coeffs.shape[0], coeffs.shape[1], width * width)

def inverse(coeffs, cosines):
    width = cosines.shape[0]
    square = coeffs.reshape(coeffs.shape[0], coeffs.shape[1], width, width)
    halfway = jnp.einsum('bcuv,ui->bicv', square, cosines, precision=lax.Precision.HIGHEST)
    field = jnp.einsum('bicv,vj->bicj', halfway, cosines, precision=lax.Precision.HIGHEST)
    return field.reshape(coeffs.shape[0] * width, coeffs.shape[1] * width)

def embed_sparse(values, freq_ids, width_sq):
    block_rows = lax.broadcasted_iota(jnp.int32, freq_ids.shape, freq_ids.ndim - 3)
    block_cols = lax.broadcasted_iota(jnp.int32, freq_ids.shape, freq_ids.ndim - 2)
    empty = jnp.zeros((freq_ids.shape[-3], freq_ids.shape[-2], width_sq), jnp.float32)
    return empty.at[block_rows, block_cols, freq_ids].add(values)

def reference(grads, momentum, picks, counts):
    cosines = dct_table(SPAN)
    slot_ids = lax.broadcasted_iota(jnp.int32, (1, 1, K_MAX), 2)

    def per_replica(accumul, item):
        partial_value, moment, chosen_ids, chosen_count = item
        summed_grad = lax.optimization_barrier(jnp.sum(partial_value.astype(jnp.float32), axis=0))
        momentum_new = 0.9 * moment + summed_grad
        coeffs = forward(momentum_new, cosines)
        live_mask = (slot_ids < chosen_count[..., None]).astype(jnp.float32)
        chosen = jnp.take_along_axis(coeffs, chosen_ids, axis=2) * live_mask
        sent_values = chosen.astype(jnp.bfloat16)
        residual_mom = momentum_new - inverse(embed_sparse(chosen, chosen_ids, SPAN * SPAN), cosines)
        accumul = accumul + embed_sparse(sent_values.astype(jnp.float32), chosen_ids, SPAN * SPAN)
        return (accumul, residual_mom)
    start_sum = jnp.zeros((RB, CC, SPAN * SPAN), jnp.float32)
    summed_coeffs, new_momentum = lax.scan(per_replica, start_sum, (grads, momentum, picks, counts))
    update = inverse(summed_coeffs, cosines).astype(jnp.bfloat16)
    return (new_momentum, update)
```

```python
import functools

import jax
import jax.numpy as jnp
import numpy as np
from jax import lax
from jax.experimental import pallas as pl
from jax.experimental.pallas import tpu as pltpu
from jax.sharding import Mesh, PartitionSpec as P

SPAN = 64
LANES = 128
QUAD = 4 * SPAN
NX, NC = 4, 2
F32, BF16 = jnp.float32, jnp.bfloat16
VMEM_LIMIT = 48 * 1024 * 1024


def split(a):
    hi = a.astype(BF16)
    return hi, (a - hi.astype(F32)).astype(BF16)


def tables():
    f = np.arange(SPAN)[:, None]
    i = np.arange(SPAN)[None, :]
    scale = np.where(f == 0, np.sqrt(1.0 / SPAN), np.sqrt(2.0 / SPAN))
    c = (scale * np.cos(np.pi * (2 * i + 1) * f / (2 * SPAN))).astype(np.float32)
    return c


def two_parts(c):
    hi = c.astype(jnp.bfloat16)
    lo = (c - hi.astype(np.float32)).astype(jnp.bfloat16)
    return hi, lo


def dot(a, b):
    return lax.dot_general(a, b, (((1,), (0,)), ((), ())), preferred_element_type=F32)


def dot_t(a, b):
    return lax.dot_general(a, b, (((1,), (1,)), ((), ())), preferred_element_type=F32)


def quads(x):
    n = x.shape[1] // QUAD
    return jnp.concatenate([x[:, QUAD * a : QUAD * (a + 1)] for a in range(n)], axis=0)


def lane_iota(shape):
    return lax.broadcasted_iota(jnp.int32, shape, len(shape) - 1)


def column_transform(x32, wide, hi_only):
    hi, lo = split(x32)
    both = dot(hi, wide)
    return both[:, :QUAD] + both[:, QUAD:] + dot(lo, hi_only)


def picked(f, ids, ct):
    lane = lane_iota((SPAN, LANES))
    known = jnp.maximum(ids, 0)
    u = jnp.broadcast_to(lax.shift_right_logical(known, 6), (SPAN, LANES))
    v = jnp.broadcast_to(jnp.bitwise_and(known, SPAN - 1), (SPAN, LANES))
    at = v + jnp.bitwise_and(lax.shift_left(lane, 1), SPAN)
    left = jnp.take_along_axis(f[:, :LANES], at, axis=1, mode="promise_in_bounds")
    right = jnp.take_along_axis(f[:, LANES:], at, axis=1, mode="promise_in_bounds")
    rows = jnp.take_along_axis(ct, u, axis=1, mode="promise_in_bounds")
    here = jnp.where(lane < SPAN, left, right)
    value = jnp.sum(here * rows, axis=0, keepdims=True)
    return jnp.where(ids >= 0, value, 0.0), rows, v


def ids_kernel(picks_ref, counts_ref, out_ref):
    n, slots = picks_ref.shape
    sub = lax.broadcasted_iota(jnp.int32, (n, n), 0)
    diag = jnp.where(sub == lane_iota((n, n)), counts_ref[...], 0)
    count = jnp.sum(diag, axis=1, keepdims=True)
    ids = jnp.where(lane_iota((n, slots)) < count, picks_ref[...], -1)
    rows = n // 4
    lines = [
        jnp.concatenate([ids[4 * a + g : 4 * a + g + 1, :] for g in range(4)], axis=1)
        for a in range(rows)
    ]
    lines.append(jnp.full((out_ref.shape[1] - rows, LANES), -1, jnp.int32))
    full = jnp.concatenate(lines, axis=0)
    for y in range(out_ref.shape[0]):
        out_ref[y] = full


def coeff_kernel(rows, me_ref, g_ref, m_ref, ids_ref, wide_ref, hi_ref, ct_ref, out_ref, f_ref):
    y = pl.program_id(0)
    both = dot(quads(g_ref[...]), wide_ref[...])
    f_ref[...] = both[:, :QUAD] + both[:, QUAD:]

    @pl.when(y == me_ref[0])
    def _():
        own = quads(0.9 * m_ref[...])
        f_ref[...] += column_transform(own, wide_ref[...], hi_ref[...])

    ct = ct_ref[...]
    per = rows // NX
    for a in range(rows):
        ids = ids_ref[0, a : a + 1, :]
        value, _, _ = picked(f_ref[SPAN * a : SPAN * (a + 1), :], ids, ct)
        out_ref[a // per, 0, a % per : a % per + 1, :] = value
        out_ref[a // per, 0, per + a % per : per + a % per + 1, :] = ids.astype(F32)
    for x in range(NX):
        out_ref[x, 0, 2 * per :, :] = jnp.zeros((8 - 2 * per, LANES), F32)


def regroup_kernel(per, got_ref, out_ref):
    leaves = got_ref.shape[1]
    values, ids = [], []
    for x in range(NX):
        total = got_ref[x, 0]
        for l in range(1, leaves):
            total = total + got_ref[x, l]
        values.append(total[:per].astype(BF16).astype(F32))
        ids.append(got_ref[x, 0][per : 2 * per])
    low = lane_iota((per, LANES)) < SPAN

    def halves(c, a, b):
        if c == 0:
            return jnp.where(low, a, pltpu.roll(b, SPAN, 1))
        return jnp.where(low, pltpu.roll(a, SPAN, 1), b)

    for c in range(NC):
        parts = [halves(c, values[2 * p], values[2 * p + 1]) for p in range(NX // 2)]
        parts += [halves(c, ids[2 * p], ids[2 * p + 1]) for p in range(NX // 2)]
        used = 2 * per * (NX // 2)
        parts.append(jnp.zeros((out_ref.shape[2] - used, LANES), F32))
        page = jnp.concatenate(parts, axis=0)
        for z in range(out_ref.shape[0]):
            out_ref[z, c] = page


def update_kernel(per, got_ref, c_hi_ref, c_lo_ref, ct_hi_ref, ct_lo_ref, out_ref):
    peers = got_ref.shape[0]
    tall = lax.broadcasted_iota(jnp.int32, (2 * SPAN, LANES), 0)
    short = lax.broadcasted_iota(jnp.int32, (SPAN, LANES), 0)
    block = lax.shift_left(jnp.bitwise_and(lax.shift_right_logical(lane_iota((1, LANES)), 5), 1), 6)

    def one_peer(n, sums):
        values = got_ref[n]
        ids = jnp.maximum(values, 0.0).astype(jnp.int32)
        us = lax.shift_right_logical(ids, 6) + block
        vs = jnp.bitwise_and(ids, SPAN - 1)
        new = []
        for a in range(per):
            left, right = [], []
            for p in range(NX // 2):
                r = p * per + a
                q = (NX // 2) * per + r
                left.append(jnp.where(tall == us[q : q + 1], values[r : r + 1], 0.0).astype(BF16))
                right.append(jnp.where(short == vs[q : q + 1], 1.0, 0.0).astype(BF16))
            new.append(
                sums[a] + dot_t(jnp.concatenate(left, axis=1), jnp.concatenate(right, axis=1))
            )
        return tuple(new)

    zero = jnp.zeros((2 * SPAN, SPAN), F32)
    sums = lax.fori_loop(0, peers, one_peer, (zero,) * per, unroll=4)
    z = jnp.concatenate(sums, axis=0)
    z_hi, z_lo = split(z)
    w = dot(z_hi, c_hi_ref[...]) + (dot(z_hi, c_lo_ref[...]) + dot(z_lo, c_hi_ref[...]))
    flat = jnp.concatenate([w[SPAN * b : SPAN * (b + 1)] for b in range(2 * per)], axis=1)
    w_hi, w_lo = split(flat)
    field = dot(ct_hi_ref[...], w_hi) + (dot(ct_lo_ref[...], w_hi) + dot(ct_hi_ref[...], w_lo))
    field = field.astype(BF16)
    for y in range(out_ref.shape[0]):
        out_ref[y] = field


def residual_kernel(step, rs_ref, m_ref, ids_ref, wide_ref, hi_ref, ct_ref, out_ref):
    first = pl.program_id(0) * step
    x = 0.9 * m_ref[...] + rs_ref[...].astype(F32)
    f = column_transform(quads(x), wide_ref[...], hi_ref[...])
    ct = ct_ref[...]
    group = lax.shift_right_logical(lane_iota((SPAN, LANES)), 5)
    for a in range(step):
        ids = ids_ref[0, pl.ds(first + a, 1), :]
        value, rows, v = picked(f[SPAN * a : SPAN * (a + 1)], ids, ct)
        cols = jnp.take_along_axis(ct, v, axis=1, mode="promise_in_bounds")
        cols = jnp.concatenate([jnp.where(group == b, cols, 0.0) for b in range(4)], axis=0)
        l_hi, l_lo = split(rows * value)
        r_hi, r_lo = split(cols)
        taken = dot_t(l_hi, r_hi) + (dot_t(l_hi, r_lo) + dot_t(l_lo, r_hi))
        out_ref[:, QUAD * a : QUAD * (a + 1)] = x[:, QUAD * a : QUAD * (a + 1)] - taken


def place_kernel(per, core_ref, mine_ref, other_ref, out_ref):
    def put(c, ref):
        for x in range(NX):
            for a in range(per):
                to = ((x * per + a) * NC + c) * LANES
                out_ref[:, to : to + LANES] = ref[x, 0, :, LANES * a : LANES * (a + 1)]

    @pl.when(core_ref[0] == 0)
    def _():
        put(0, mine_ref)
        put(1, other_ref)

    @pl.when(core_ref[0] != 0)
    def _():
        put(1, mine_ref)
        put(0, other_ref)


def call(kernel, out_shape, **kw):
    return pl.pallas_call(
        kernel,
        out_shape=out_shape,
        compiler_params=pltpu.CompilerParams(vmem_limit_bytes=VMEM_LIMIT),
        **kw,
    )


def on_device(nz, leaves, grads, momentum, picks, counts):
    c = tables()
    c_hi, c_lo = two_parts(c)
    ct_hi, ct_lo = two_parts(np.ascontiguousarray(c.T))
    eye = np.eye(4, dtype=np.float32)
    bd_hi = np.kron(eye, ct_hi.astype(np.float32)).astype(jnp.bfloat16)
    bd_lo = np.kron(eye, ct_lo.astype(np.float32)).astype(jnp.bfloat16)
    wide = jnp.asarray(np.concatenate([bd_hi, bd_lo], axis=1))
    bd_hi = jnp.asarray(bd_hi)
    ct = jnp.asarray(np.concatenate([c.T, c.T], axis=1))

    columns = grads.shape[3]
    own_cols = columns // leaves
    blocks = picks.shape[2]
    rows = blocks // 4
    per = rows // NX
    peers = nz * NC
    g = grads.reshape(SPAN, columns)
    m = momentum.reshape(SPAN, own_cols)
    leaf = lax.axis_index("leaf")
    core = lax.axis_index("core")
    whole = pl.BlockSpec(memory_space=pltpu.VMEM)
    scalar = pl.BlockSpec(memory_space=pltpu.SMEM)

    summed = lax.psum_scatter(g, "leaf", scatter_dimension=1, tiled=True)

    own_ids = call(ids_kernel, jax.ShapeDtypeStruct((leaves, 16, LANES), jnp.int32))(
        picks.reshape(blocks, picks.shape[3]), counts.reshape(1, blocks)
    )
    all_ids = lax.all_to_all(own_ids, "leaf", 0, 0, tiled=True)

    partial = call(
        functools.partial(coeff_kernel, rows),
        jax.ShapeDtypeStruct((NX, leaves, 8, LANES), F32),
        grid=(leaves,),
        in_specs=[
            scalar,
            pl.BlockSpec((SPAN, own_cols), lambda y: (0, y)),
            whole,
            pl.BlockSpec((1, 16, LANES), lambda y: (y, 0, 0)),
            whole,
            whole,
            whole,
        ],
        out_specs=pl.BlockSpec((NX, 1, 8, LANES), lambda y: (0, y, 0, 0)),
        scratch_shapes=[pltpu.VMEM((rows * SPAN, QUAD), F32)],
    )(leaf.reshape(1), g, m, all_ids, wide, bd_hi, ct)
    got = lax.all_to_all(
        partial.reshape(NX * leaves, 8, LANES), ("x", "leaf"), 0, 0, tiled=True
    )

    sent = call(
        functools.partial(regroup_kernel, per),
        jax.ShapeDtypeStruct((nz, NC, 16, LANES), F32),
    )(got.reshape(NX, leaves, 8, LANES))
    got = lax.all_to_all(sent.reshape(peers, 16, LANES), ("z", "core"), 0, 0, tiled=True)

    wide_cols = 2 * per * SPAN
    field = call(
        functools.partial(update_kernel, per),
        jax.ShapeDtypeStruct((leaves, SPAN, wide_cols), BF16),
    )(got, jnp.asarray(c_hi), jnp.asarray(c_lo), jnp.asarray(ct_hi), jnp.asarray(ct_lo))
    field = lax.all_to_all(field, "leaf", 0, 0, tiled=True)
    field = jnp.broadcast_to(field[None], (NX,) + field.shape)
    mine = lax.all_to_all(field, "x", 0, 0, tiled=True)
    summed, mine = lax.optimization_barrier((summed, mine))
    other = lax.ppermute(mine, "core", [(0, 1), (1, 0)])

    step = 3
    residual = call(
        functools.partial(residual_kernel, step),
        jax.ShapeDtypeStruct((SPAN, own_cols), F32),
        grid=(rows // step,),
        in_specs=[
            pl.BlockSpec((SPAN, step * QUAD), lambda i: (0, i)),
            pl.BlockSpec((SPAN, step * QUAD), lambda i: (0, i)),
            pl.BlockSpec((1, 16, LANES), lambda i: (0, 0, 0)),
            whole,
            whole,
            whole,
        ],
        out_specs=pl.BlockSpec((SPAN, step * QUAD), lambda i: (0, i)),
        cost_estimate=pl.CostEstimate(flops=10**9, bytes_accessed=8 * 10**6, transcendentals=0),
    )(summed, m, own_ids, wide, bd_hi, ct)

    update = call(
        functools.partial(place_kernel, per),
        jax.ShapeDtypeStruct((SPAN, columns), BF16),
        grid=(leaves,),
        in_specs=[
            scalar,
            pl.BlockSpec((NX, 1, SPAN, wide_cols), lambda y: (0, y, 0, 0)),
            pl.BlockSpec((NX, 1, SPAN, wide_cols), lambda y: (0, y, 0, 0)),
        ],
        out_specs=pl.BlockSpec((SPAN, own_cols), lambda y: (0, y)),
    )(core.reshape(1), mine, other)
    return (residual[None], update)


def solution(mesh):
    reps, leaves = mesh.devices.shape
    nz = reps // (NX * NC)
    fine = Mesh(mesh.devices.reshape(NX, nz, NC, leaves), ("x", "z", "core", "leaf"))
    rep = ("x", "z", "core")
    placed = (
        P(rep, "leaf", None, None),
        P(rep, None, "leaf"),
        P(rep, None, "leaf", None),
        P(rep, None, "leaf"),
    )
    return jax.shard_map(
        functools.partial(on_device, nz, leaves),
        mesh=fine,
        in_specs=placed,
        out_specs=(P(rep, None, "leaf"), P()),
        check_vma=False,
    )
```

```python
import functools

import jax
import jax.numpy as jnp
import numpy as np
from jax import lax
from jax.experimental import pallas as pl
from jax.experimental.pallas import tpu as pltpu
from jax.sharding import Mesh, PartitionSpec as P

SPAN = 64
LANES = 128
QUAD = 4 * SPAN
NX, NC = 4, 2
F32, BF16 = jnp.float32, jnp.bfloat16
VMEM_LIMIT = 48 * 1024 * 1024


def split(a):
    hi = a.astype(BF16)
    return hi, (a - hi.astype(F32)).astype(BF16)


def tables():
    f = np.arange(SPAN)[:, None]
    i = np.arange(SPAN)[None, :]
    scale = np.where(f == 0, np.sqrt(1.0 / SPAN), np.sqrt(2.0 / SPAN))
    c = (scale * np.cos(np.pi * (2 * i + 1) * f / (2 * SPAN))).astype(np.float32)
    return c


def two_parts(c):
    hi = c.astype(jnp.bfloat16)
    lo = (c - hi.astype(np.float32)).astype(jnp.bfloat16)
    return hi, lo


def dot(a, b):
    return lax.dot_general(a, b, (((1,), (0,)), ((), ())), preferred_element_type=F32)


def dot_t(a, b):
    return lax.dot_general(a, b, (((1,), (1,)), ((), ())), preferred_element_type=F32)


def quads(x):
    n = x.shape[1] // QUAD
    return jnp.concatenate([x[:, QUAD * a : QUAD * (a + 1)] for a in range(n)], axis=0)


def lane_iota(shape):
    return lax.broadcasted_iota(jnp.int32, shape, len(shape) - 1)


def column_transform(x32, wide, hi_only):
    hi, lo = split(x32)
    both = dot(hi, wide)
    return both[:, :QUAD] + both[:, QUAD:] + dot(lo, hi_only)


def picked(f, ids, ct):
    lane = lane_iota((SPAN, LANES))
    known = jnp.maximum(ids, 0)
    u = jnp.broadcast_to(lax.shift_right_logical(known, 6), (SPAN, LANES))
    v = jnp.broadcast_to(jnp.bitwise_and(known, SPAN - 1), (SPAN, LANES))
    at = v + jnp.bitwise_and(lax.shift_left(lane, 1), SPAN)
    left = jnp.take_along_axis(f[:, :LANES], at, axis=1, mode="promise_in_bounds")
    right = jnp.take_along_axis(f[:, LANES:], at, axis=1, mode="promise_in_bounds")
    rows = jnp.take_along_axis(ct, u, axis=1, mode="promise_in_bounds")
    here = jnp.where(lane < SPAN, left, right)
    value = jnp.sum(here * rows, axis=0, keepdims=True)
    return jnp.where(ids >= 0, value, 0.0), rows, v


def fetch(pairs, sems):
    copies = [pltpu.make_async_copy(src, dst, sems.at[i]) for i, (src, dst) in enumerate(pairs)]
    for copy in copies:
        copy.start()
    return copies


def ids_kernel(picks_hbm, counts_hbm, out_ref, picks_ref, counts_ref, sems):
    for copy in fetch([(picks_hbm, picks_ref), (counts_hbm, counts_ref)], sems):
        copy.wait()
    slots, n = picks_ref.shape
    slot = lax.broadcasted_iota(jnp.int32, (slots, n), 0)
    ids = jnp.where(slot < counts_ref[...], picks_ref[...], -1).T
    rows = n // 4
    lines = [
        jnp.concatenate([ids[4 * a + g : 4 * a + g + 1, :] for g in range(4)], axis=1)
        for a in range(rows)
    ]
    lines.append(jnp.full((out_ref.shape[1] - rows, LANES), -1, jnp.int32))
    full = jnp.concatenate(lines, axis=0)
    for y in range(out_ref.shape[0]):
        out_ref[y] = full


def dense_kernel(leaves, me_ref, g_hbm, m_hbm, wide_hbm, ct_hbm, f_ref, ct_ref, buf, m_ref, wide_ref, sems):
    cols = g_hbm.shape[1] // leaves
    pairs = [(wide_hbm, wide_ref)]
    pairs += [(g_hbm.at[:, y * cols : (y + 1) * cols], buf.at[y]) for y in range(leaves)]
    pairs += [(m_hbm, m_ref), (ct_hbm, ct_ref)]
    copies = fetch(pairs, sems)
    copies[0].wait()
    for y in range(leaves):
        copies[1 + y].wait()
        both = dot(quads(buf[y]), wide_ref[...])
        f_ref[y] = both[:, :QUAD] + both[:, QUAD:]
    copies[leaves + 1].wait()
    me = me_ref[0]
    f_ref[me] += column_transform(quads(0.9 * m_ref[...]), wide_ref[...], wide_ref[:, :QUAD])
    copies[leaves + 2].wait()


def coeff_kernel(rows, f_ref, ids_ref, ct_ref, out_ref):
    ct = ct_ref[...]
    per = rows // NX

    def one_leaf(y, carry):
        for a in range(rows):
            ids = ids_ref[y, a : a + 1, :]
            value, _, _ = picked(f_ref[y, SPAN * a : SPAN * (a + 1), :], ids, ct)
            out_ref[a // per, y, a % per : a % per + 1, :] = value
            out_ref[a // per, y, per + a % per : per + a % per + 1, :] = ids.astype(F32)
        for x in range(NX):
            out_ref[x, y, 2 * per :, :] = jnp.zeros((8 - 2 * per, LANES), F32)
        return carry

    lax.fori_loop(0, f_ref.shape[0], one_leaf, 0)


def regroup_kernel(per, got_ref, out_ref):
    leaves = got_ref.shape[1]
    values, ids = [], []
    for x in range(NX):
        total = got_ref[x, 0]
        for l in range(1, leaves):
            total = total + got_ref[x, l]
        values.append(total[:per].astype(BF16).astype(F32))
        ids.append(got_ref[x, 0][per : 2 * per])
    low = lane_iota((1, LANES)) < SPAN

    def pair(of, p, q):
        row, half = q // 2, q % 2
        a, b = of[2 * p][row : row + 1], of[2 * p + 1][row : row + 1]
        if half == 0:
            return jnp.where(low, a, pltpu.roll(b, SPAN, 1))
        return jnp.where(low, pltpu.roll(a, SPAN, 1), b)

    for c in range(NC):
        lines = [pair(of, p, c * per + j) for of in (values, ids) for p in range(NX // 2) for j in range(per)]
        lines.append(jnp.zeros((out_ref.shape[2] - len(lines), LANES), F32))
        page = jnp.concatenate(lines, axis=0)
        for z in range(out_ref.shape[0]):
            out_ref[z, c] = page


def update_kernel(per, got_ref, tab_hbm, out_ref, tab_ref, sems):
    (copy,) = fetch([(tab_hbm, tab_ref)], sems)
    peers = got_ref.shape[0]
    tall = lax.broadcasted_iota(jnp.int32, (2 * SPAN, LANES), 0)
    short = lax.broadcasted_iota(jnp.int32, (SPAN, LANES), 0)
    block = lax.shift_left(jnp.bitwise_and(lax.shift_right_logical(lane_iota((1, LANES)), 5), 1), 6)

    def one_peer(n, sums):
        values = got_ref[n]
        ids = jnp.maximum(values, 0.0).astype(jnp.int32)
        us = lax.shift_right_logical(ids, 6) + block
        vs = jnp.bitwise_and(ids, SPAN - 1)
        new = []
        for a in range(per):
            left, right = [], []
            for p in range(NX // 2):
                r = p * per + a
                q = (NX // 2) * per + r
                left.append(jnp.where(tall == us[q : q + 1], values[r : r + 1], 0.0).astype(BF16))
                right.append(jnp.where(short == vs[q : q + 1], 1.0, 0.0).astype(BF16))
            new.append(
                sums[a] + dot_t(jnp.concatenate(left, axis=1), jnp.concatenate(right, axis=1))
            )
        return tuple(new)

    zero = jnp.zeros((2 * SPAN, SPAN), F32)
    sums = lax.fori_loop(0, peers, one_peer, (zero,) * per, unroll=4)
    z = jnp.concatenate(sums, axis=0)
    z_hi, z_lo = split(z)
    copy.wait()
    c_hi, c_lo, ct_hi, ct_lo = [tab_ref[i] for i in range(4)]
    w = dot(z_hi, c_hi) + (dot(z_hi, c_lo) + dot(z_lo, c_hi))
    flat = jnp.concatenate([w[SPAN * b : SPAN * (b + 1)] for b in range(2 * per)], axis=1)
    w_hi, w_lo = split(flat)
    field = dot(ct_hi, w_hi) + (dot(ct_lo, w_hi) + dot(ct_hi, w_lo))
    field = field.astype(BF16)
    for y in range(out_ref.shape[0]):
        out_ref[y] = field


def residual_kernel(step, sum_ref, m_ref, ids_ref, wide_ref, ct_ref, out_ref):
    first = pl.program_id(0) * step
    x = 0.9 * m_ref[...] + sum_ref[...].astype(F32)
    f = column_transform(quads(x), wide_ref[...], wide_ref[:, :QUAD])
    ct = ct_ref[...]
    group = lax.shift_right_logical(lane_iota((SPAN, LANES)), 5)
    for a in range(step):
        ids = ids_ref[0, pl.ds(first + a, 1), :]
        value, rows, v = picked(f[SPAN * a : SPAN * (a + 1)], ids, ct)
        cols = jnp.take_along_axis(ct, v, axis=1, mode="promise_in_bounds")
        cols = jnp.concatenate([jnp.where(group == b, cols, 0.0) for b in range(4)], axis=0)
        l_hi, l_lo = split(rows * value)
        r_hi, r_lo = split(cols)
        taken = dot_t(l_hi, r_hi) + (dot_t(l_hi, r_lo) + dot_t(l_lo, r_hi))
        out_ref[:, QUAD * a : QUAD * (a + 1)] = x[:, QUAD * a : QUAD * (a + 1)] - taken


def place_kernel(core_ref, field_hbm, _, out_hbm, sem):
    nx, leaves, _, cols = field_hbm.shape
    c = core_ref[0]
    copies = []
    for y in range(leaves):
        for x in range(nx):
            at = pl.multiple_of(((y * nx + x) * NC + c) * cols, LANES)
            copies.append(
                pltpu.make_async_copy(field_hbm.at[x, y], out_hbm.at[:, pl.ds(at, cols)], sem.at[y * nx + x])
            )
    for copy in copies:
        copy.start()
    for copy in copies:
        copy.wait()


def place_first(kernel, core_ref, field_hbm, out_hbm, sem):
    kernel(core_ref, field_hbm, None, out_hbm, sem)


def call(kernel, out_shape, vmem=VMEM_LIMIT, **kw):
    return pl.pallas_call(
        kernel,
        out_shape=out_shape,
        compiler_params=pltpu.CompilerParams(vmem_limit_bytes=vmem),
        **kw,
    )


def on_device(nz, leaves, grads, momentum, picks, counts):
    c = tables()
    c_hi, c_lo = two_parts(c)
    ct_hi, ct_lo = two_parts(np.ascontiguousarray(c.T))
    eye = np.eye(4, dtype=np.float32)
    bd_hi = np.kron(eye, ct_hi.astype(np.float32)).astype(jnp.bfloat16)
    bd_lo = np.kron(eye, ct_lo.astype(np.float32)).astype(jnp.bfloat16)
    wide = jnp.asarray(np.concatenate([bd_hi, bd_lo], axis=1))
    tab = jnp.asarray(np.stack([c_hi, c_lo, ct_hi, ct_lo]))
    ct = jnp.asarray(np.concatenate([c.T, c.T], axis=1))

    columns = grads.shape[3]
    own_cols = columns // leaves
    blocks, slots = picks.shape[2:]
    rows = blocks // 4
    per = rows // NX
    peers = nz * NC
    g = grads.reshape(SPAN, columns)
    m = momentum.reshape(SPAN, own_cols)
    leaf = lax.axis_index("leaf")
    core = lax.axis_index("core")
    whole = pl.BlockSpec(memory_space=pltpu.VMEM)
    scalar = pl.BlockSpec(memory_space=pltpu.SMEM)
    hbm = pl.BlockSpec(memory_space=pltpu.HBM)
    anywhere = pl.BlockSpec(memory_space=pl.ANY)
    dma = pltpu.SemaphoreType.DMA

    summed = lax.psum_scatter(g, "leaf", scatter_dimension=1, tiled=True)

    own_ids = call(
        ids_kernel,
        jax.ShapeDtypeStruct((leaves, 16, LANES), jnp.int32),
        vmem=62 * 1024 * 1024,
        in_specs=[hbm, hbm],
        scratch_shapes=[
            pltpu.VMEM((slots, blocks), jnp.int32),
            pltpu.VMEM((1, blocks), jnp.int32),
            dma((2,)),
        ],
    )(picks.reshape(blocks, slots).T, counts.reshape(1, blocks))
    all_ids = lax.all_to_all(own_ids, "leaf", 0, 0, tiled=True)

    f, ct = call(
        functools.partial(dense_kernel, leaves),
        (
            jax.ShapeDtypeStruct((leaves, rows * SPAN, QUAD), F32),
            jax.ShapeDtypeStruct(ct.shape, F32),
        ),
        in_specs=[scalar, hbm, hbm, hbm, hbm],
        out_specs=(whole, whole),
        scratch_shapes=[
            pltpu.VMEM((leaves, SPAN, own_cols), BF16),
            pltpu.VMEM((SPAN, own_cols), F32),
            pltpu.VMEM(wide.shape, BF16),
            dma((leaves + 3,)),
        ],
        cost_estimate=pl.CostEstimate(flops=2 * 10**9, bytes_accessed=16 * 10**6, transcendentals=0),
    )(leaf.reshape(1), g, m, wide, ct)

    partial = call(
        functools.partial(coeff_kernel, rows),
        jax.ShapeDtypeStruct((NX, leaves, 8, LANES), F32),
    )(f, all_ids, ct)
    got = lax.all_to_all(
        partial.reshape(NX * leaves, 8, LANES), ("x", "leaf"), 0, 0, tiled=True
    )

    sent = call(
        functools.partial(regroup_kernel, per),
        jax.ShapeDtypeStruct((nz, NC, 16, LANES), F32),
    )(got.reshape(NX, leaves, 8, LANES))
    got = lax.all_to_all(sent.reshape(peers, 16, LANES), ("z", "core"), 0, 0, tiled=True)

    wide_cols = 2 * per * SPAN
    field = call(
        functools.partial(update_kernel, per),
        jax.ShapeDtypeStruct((leaves, SPAN, wide_cols), BF16),
        in_specs=[whole, hbm],
        scratch_shapes=[pltpu.VMEM(tab.shape, BF16), dma((1,))],
    )(got, tab)
    summed, field = lax.optimization_barrier((summed, field))
    field = lax.all_to_all(field, "leaf", 0, 0, tiled=True)
    field = jnp.broadcast_to(field[None], (NX,) + field.shape)
    mine = lax.all_to_all(field, "x", 0, 0, tiled=True)
    step = 3
    residual = call(
        functools.partial(residual_kernel, step),
        jax.ShapeDtypeStruct((SPAN, own_cols), F32),
        grid=(rows // step,),
        in_specs=[
            pl.BlockSpec((SPAN, step * QUAD), lambda i: (0, i)),
            pl.BlockSpec((SPAN, step * QUAD), lambda i: (0, i)),
            pl.BlockSpec((1, 16, LANES), lambda i: (0, 0, 0)),
            whole,
            whole,
        ],
        out_specs=pl.BlockSpec((SPAN, step * QUAD), lambda i: (0, i)),
        cost_estimate=pl.CostEstimate(flops=10**9, bytes_accessed=16 * 10**6, transcendentals=0),
    )(summed, m, own_ids, wide, ct)

    residual, mine = lax.optimization_barrier((residual, mine))
    other = lax.ppermute(mine, "core", [(0, 1), (1, 0)])

    def place(who, piece, base):
        more = {} if base is None else {"input_output_aliases": {2: 0}}
        operands = (who.reshape(1), piece) + (() if base is None else (base,))
        return call(
            place_kernel if base is not None else functools.partial(place_first, place_kernel),
            jax.ShapeDtypeStruct((SPAN, columns), BF16),
            in_specs=[scalar] + [anywhere] * (len(operands) - 1),
            out_specs=hbm,
            scratch_shapes=[dma((NX * leaves,))],
            cost_estimate=pl.CostEstimate(flops=0, bytes_accessed=4 * 10**6, transcendentals=0),
            **more,
        )(*operands)

    update = place(core, mine, None)
    update = place(1 - core, other, update)
    return (residual[None], update)


def solution(mesh):
    reps, leaves = mesh.devices.shape
    nz = reps // (NX * NC)
    fine = Mesh(mesh.devices.reshape(NX, nz, NC, leaves), ("x", "z", "core", "leaf"))
    rep = ("x", "z", "core")
    placed = (
        P(rep, "leaf", None, None),
        P(rep, None, "leaf"),
        P(rep, None, "leaf", None),
        P(rep, None, "leaf"),
    )
    return jax.shard_map(
        functools.partial(on_device, nz, leaves),
        mesh=fine,
        in_specs=placed,
        out_specs=(P(rep, None, "leaf"), P()),
        check_vma=False,
    )
```

```python
import functools

import jax
import jax.numpy as jnp
import numpy as np
from jax import lax
from jax.experimental import pallas as pl
from jax.experimental.pallas import tpu as pltpu
from jax.sharding import Mesh, PartitionSpec as P

SPAN = 64
LANES = 128
QUAD = 4 * SPAN
NX, NC = 4, 2
F32, BF16 = jnp.float32, jnp.bfloat16
VMEM_LIMIT = 24 * 1024 * 1024


def split(a):
    hi = a.astype(BF16)
    return hi, (a - hi.astype(F32)).astype(BF16)


def tables():
    f = np.arange(SPAN)[:, None]
    i = np.arange(SPAN)[None, :]
    scale = np.where(f == 0, np.sqrt(1.0 / SPAN), np.sqrt(2.0 / SPAN))
    c = (scale * np.cos(np.pi * (2 * i + 1) * f / (2 * SPAN))).astype(np.float32)
    return c


def two_parts(c):
    hi = c.astype(jnp.bfloat16)
    lo = (c - hi.astype(np.float32)).astype(jnp.bfloat16)
    return hi, lo


def dot(a, b):
    return lax.dot_general(a, b, (((1,), (0,)), ((), ())), preferred_element_type=F32)


def dot_t(a, b):
    return lax.dot_general(a, b, (((1,), (1,)), ((), ())), preferred_element_type=F32)


def quads(x):
    n = x.shape[1] // QUAD
    return jnp.concatenate([x[:, QUAD * a : QUAD * (a + 1)] for a in range(n)], axis=0)


def lane_iota(shape):
    return lax.broadcasted_iota(jnp.int32, shape, len(shape) - 1)


def column_transform(x32, wide, hi_only):
    hi, lo = split(x32)
    both = dot(hi, wide)
    return both[:, :QUAD] + both[:, QUAD:] + dot(lo, hi_only)


def picked(f, ids, ct):
    lane = lane_iota((SPAN, LANES))
    known = jnp.maximum(ids, 0)
    u = jnp.broadcast_to(lax.shift_right_logical(known, 6), (SPAN, LANES))
    v = jnp.broadcast_to(jnp.bitwise_and(known, SPAN - 1), (SPAN, LANES))
    at = v + jnp.bitwise_and(lax.shift_left(lane, 1), SPAN)
    left = jnp.take_along_axis(f[:, :LANES], at, axis=1, mode="promise_in_bounds")
    right = jnp.take_along_axis(f[:, LANES:], at, axis=1, mode="promise_in_bounds")
    rows = jnp.take_along_axis(ct, u, axis=1, mode="promise_in_bounds")
    here = jnp.where(lane < SPAN, left, right)
    value = jnp.sum(here * rows, axis=0, keepdims=True)
    return jnp.where(ids >= 0, value, 0.0), rows, v


def fetch(pairs, sems):
    copies = [pltpu.make_async_copy(src, dst, sems.at[i]) for i, (src, dst) in enumerate(pairs)]
    for copy in copies:
        copy.start()
    return copies


def ids_kernel(picks_hbm, counts_hbm, out_ref, picks_ref, counts_ref, sems):
    for copy in fetch([(picks_hbm, picks_ref), (counts_hbm, counts_ref)], sems):
        copy.wait()
    slots, n = picks_ref.shape
    slot = lax.broadcasted_iota(jnp.int32, (slots, n), 0)
    ids = jnp.where(slot < counts_ref[...], picks_ref[...], -1).T
    rows = n // 4
    lines = [
        jnp.concatenate([ids[4 * a + g : 4 * a + g + 1, :] for g in range(4)], axis=1)
        for a in range(rows)
    ]
    lines.append(jnp.full((out_ref.shape[1] - rows, LANES), -1, jnp.int32))
    full = jnp.concatenate(lines, axis=0)
    for y in range(out_ref.shape[0]):
        out_ref[y] = full


def dense_kernel(
    leaves, me_ref, g_hbm, m_hbm, wide_hbm, f_hbm, buf, m_ref, wide_ref, f_ref, sems, outs
):
    cols = g_hbm.shape[1] // leaves
    pairs = [(wide_hbm, wide_ref)]
    pairs += [(g_hbm.at[:, y * cols : (y + 1) * cols], buf.at[y]) for y in range(leaves)]
    pairs += [(m_hbm, m_ref)]
    copies = fetch(pairs, sems)
    copies[0].wait()
    me = me_ref[0]
    back = []
    for y in range(leaves):
        copies[1 + y].wait()
        both = dot(quads(buf[y]), wide_ref[...])
        f_ref[y] = both[:, :QUAD] + both[:, QUAD:]
        if y == 0:
            copies[leaves + 1].wait()

        @pl.when(me == y)
        def _():
            own = column_transform(quads(0.9 * m_ref[...]), wide_ref[...], wide_ref[:, :QUAD])
            f_ref[y] += own

        copy = pltpu.make_async_copy(f_ref.at[y], f_hbm.at[y], outs.at[y])
        copy.start()
        back.append(copy)
    for copy in back:
        copy.wait()


def coeff_kernel(rows, f_hbm, ids_ref, ct_hbm, out_ref, f_ref, ct_ref, sems):
    leaves = f_hbm.shape[0]
    pairs = [(ct_hbm, ct_ref)] + [(f_hbm.at[y], f_ref.at[y]) for y in range(leaves)]
    first, *copies = fetch(pairs, sems)
    first.wait()
    ct = ct_ref[...]
    for y in range(leaves):
        copies[y].wait()
        for a in range(rows):
            value, _, _ = picked(f_ref[y, SPAN * a : SPAN * (a + 1), :], ids_ref[y, a : a + 1, :], ct)
            out_ref[y, a : a + 1, :] = value
        out_ref[y, rows:, :] = jnp.zeros((out_ref.shape[1] - rows, LANES), F32)


def regroup_kernel(per, got_ref, ids_ref, out_ref):
    total = got_ref[0]
    for l in range(1, got_ref.shape[0]):
        total = total + got_ref[l]
    total = total.astype(BF16).astype(F32)
    ids = jnp.maximum(ids_ref[0], 0).astype(F32)
    low = lane_iota((1, LANES)) < SPAN
    for x in range(NX):
        for c in range(NC):
            keep = low if c == 0 else jnp.logical_not(low)
            full, half = per * x + (per - 1) * c, per * x + 1
            lines = []
            for of in (total, ids):
                lines += [of[full : full + 1], jnp.where(keep, of[half : half + 1], 0.0)]
            page = jnp.concatenate(lines, axis=0)
            for z in range(out_ref.shape[1]):
                out_ref[x, z, c] = page


def update_kernel(per, core_ref, got_ref, tab_hbm, out_ref, tab_ref, sems):
    (copy,) = fetch([(tab_hbm, tab_ref)], sems)
    peers = got_ref.shape[0]
    tall = lax.broadcasted_iota(jnp.int32, (2 * SPAN, LANES), 0)
    short = lax.broadcasted_iota(jnp.int32, (SPAN, LANES), 0)
    block = lax.shift_left(jnp.bitwise_and(lax.shift_right_logical(lane_iota((1, LANES)), 5), 1), 6)
    low = lane_iota((2, LANES)) < SPAN

    def two_peers(n):
        a, b = got_ref[n], got_ref[n + 1]
        turned_a, turned_b = pltpu.roll(a, SPAN, 1), pltpu.roll(b, SPAN, 1)
        pick = [jnp.concatenate([v[0:1], v[2:3]], axis=0) for v in (a, turned_a, b, turned_b)]
        first = jnp.where(low, pick[0], pick[3])
        second = jnp.where(low, pick[1], pick[2])
        third = jnp.concatenate([a[1:2] + turned_b[1:2], a[3:4] + turned_b[3:4]], axis=0)
        return first, second, third

    def four_peers(n, sums):
        pairs = [two_peers(4 * n), two_peers(4 * n + 2)]
        new = []
        for a in range(per):
            left, right = [], []
            for lines in pairs:
                value, ids = lines[a][0:1], lines[a][1:2].astype(jnp.int32)
                u = lax.shift_right_logical(ids, 6) + block
                v = jnp.bitwise_and(ids, SPAN - 1)
                left.append(jnp.where(tall == u, value, 0.0).astype(BF16))
                right.append(jnp.where(short == v, 1.0, 0.0).astype(BF16))
            new.append(
                sums[a] + dot_t(jnp.concatenate(left, axis=1), jnp.concatenate(right, axis=1))
            )
        return tuple(new)

    zero = jnp.zeros((2 * SPAN, SPAN), F32)
    sums = lax.fori_loop(0, peers // 4, four_peers, (zero,) * per, unroll=True)
    z = jnp.concatenate(sums, axis=0)
    z_hi, z_lo = split(z)
    copy.wait()
    c_hi, c_lo, ct_hi, ct_lo = [tab_ref[i] for i in range(4)]
    w = dot(z_hi, c_hi) + (dot(z_hi, c_lo) + dot(z_lo, c_hi))
    flat = jnp.concatenate([w[SPAN * b : SPAN * (b + 1)] for b in range(2 * per)], axis=1)
    w_hi, w_lo = split(flat)
    field = dot(ct_hi, w_hi) + (dot(ct_lo, w_hi) + dot(ct_hi, w_lo))
    edge = 2 * LANES
    turned = jnp.concatenate([field[:, edge:], field[:, :edge]], axis=1)
    field = jnp.where(core_ref[0] == 0, field, turned).astype(BF16)
    for y in range(out_ref.shape[0]):
        out_ref[y] = field


def residual_kernel(step, sum_ref, m_ref, ids_ref, wide_ref, ct_ref, out_ref):
    first = pl.program_id(0) * step
    x = 0.9 * m_ref[...] + sum_ref[...].astype(F32)
    f = column_transform(quads(x), wide_ref[...], wide_ref[:, :QUAD])
    ct = ct_ref[...]
    group = lax.shift_right_logical(lane_iota((SPAN, LANES)), 5)
    for a in range(step):
        ids = ids_ref[0, pl.ds(first + a, 1), :]
        value, rows, v = picked(f[SPAN * a : SPAN * (a + 1)], ids, ct)
        cols = jnp.take_along_axis(ct, v, axis=1, mode="promise_in_bounds")
        cols = jnp.concatenate([jnp.where(group == b, cols, 0.0) for b in range(4)], axis=0)
        l_hi, l_lo = split(rows * value)
        r_hi, r_lo = split(cols)
        taken = dot_t(l_hi, r_hi) + (dot_t(l_hi, r_lo) + dot_t(l_lo, r_hi))
        out_ref[:, QUAD * a : QUAD * (a + 1)] = x[:, QUAD * a : QUAD * (a + 1)] - taken


def place_kernel(core_ref, field_hbm, _, out_hbm, sem):
    nx, leaves, _, cols = field_hbm.shape
    c = core_ref[0]
    copies = []
    for y in range(leaves):
        for x in range(nx):
            at = pl.multiple_of(((y * nx + x) * NC + c) * cols, LANES)
            copies.append(
                pltpu.make_async_copy(field_hbm.at[x, y], out_hbm.at[:, pl.ds(at, cols)], sem.at[y * nx + x])
            )
    for copy in copies:
        copy.start()
    for copy in copies:
        copy.wait()


def place_first(kernel, core_ref, field_hbm, out_hbm, sem):
    kernel(core_ref, field_hbm, None, out_hbm, sem)


def call(kernel, out_shape, vmem=VMEM_LIMIT, **kw):
    return pl.pallas_call(
        kernel,
        out_shape=out_shape,
        compiler_params=pltpu.CompilerParams(vmem_limit_bytes=vmem),
        **kw,
    )


def on_device(nz, leaves, grads, momentum, picks, counts):
    c = tables()
    c_hi, c_lo = two_parts(c)
    ct_hi, ct_lo = two_parts(np.ascontiguousarray(c.T))
    eye = np.eye(4, dtype=np.float32)
    bd_hi = np.kron(eye, ct_hi.astype(np.float32)).astype(jnp.bfloat16)
    bd_lo = np.kron(eye, ct_lo.astype(np.float32)).astype(jnp.bfloat16)
    wide = jnp.asarray(np.concatenate([bd_hi, bd_lo], axis=1))
    tab = jnp.asarray(np.stack([c_hi, c_lo, ct_hi, ct_lo]))
    ct = jnp.asarray(np.concatenate([c.T, c.T], axis=1))

    columns = grads.shape[3]
    own_cols = columns // leaves
    blocks, slots = picks.shape[2:]
    rows = blocks // 4
    per = rows // NX
    peers = nz * NC
    g = grads.reshape(SPAN, columns)
    m = momentum.reshape(SPAN, own_cols)
    leaf = lax.axis_index("leaf")
    core = lax.axis_index("core")
    whole = pl.BlockSpec(memory_space=pltpu.VMEM)
    scalar = pl.BlockSpec(memory_space=pltpu.SMEM)
    hbm = pl.BlockSpec(memory_space=pltpu.HBM)
    anywhere = pl.BlockSpec(memory_space=pl.ANY)
    dma = pltpu.SemaphoreType.DMA

    summed = lax.psum_scatter(g, "leaf", scatter_dimension=1, tiled=True)

    own_ids = call(
        ids_kernel,
        jax.ShapeDtypeStruct((leaves, 16, LANES), jnp.int32),
        vmem=62 * 1024 * 1024,
        in_specs=[hbm, hbm],
        scratch_shapes=[
            pltpu.VMEM((slots, blocks), jnp.int32),
            pltpu.VMEM((1, blocks), jnp.int32),
            dma((2,)),
        ],
    )(picks.reshape(blocks, slots).T, counts.reshape(1, blocks))
    all_ids = lax.all_to_all(own_ids, "leaf", 0, 0, tiled=True)

    f = call(
        functools.partial(dense_kernel, leaves),
        jax.ShapeDtypeStruct((leaves, rows * SPAN, QUAD), F32),
        vmem=56 * 1024 * 1024,
        in_specs=[scalar, hbm, hbm, hbm],
        out_specs=hbm,
        scratch_shapes=[
            pltpu.VMEM((leaves, SPAN, own_cols), BF16),
            pltpu.VMEM((SPAN, own_cols), F32),
            pltpu.VMEM(wide.shape, BF16),
            pltpu.VMEM((leaves, rows * SPAN, QUAD), F32),
            dma((leaves + 2,)),
            dma((leaves,)),
        ],
        cost_estimate=pl.CostEstimate(flops=2 * 10**9, bytes_accessed=16 * 10**6, transcendentals=0),
    )(leaf.reshape(1), g, m, wide)

    partial = call(
        functools.partial(coeff_kernel, rows),
        jax.ShapeDtypeStruct((leaves, 16, LANES), F32),
        vmem=58 * 1024 * 1024,
        in_specs=[hbm, whole, hbm],
        scratch_shapes=[
            pltpu.VMEM((leaves, rows * SPAN, QUAD), F32),
            pltpu.VMEM(ct.shape, F32),
            dma((leaves + 1,)),
        ],
    )(f, all_ids, ct)
    got = lax.all_to_all(partial, "leaf", 0, 0, tiled=True)

    sent = call(
        functools.partial(regroup_kernel, per),
        jax.ShapeDtypeStruct((NX, nz, NC, 4, LANES), F32),
    )(got, own_ids)
    got = lax.all_to_all(
        sent.reshape(NX * peers, 4, LANES), ("x", "z", "core"), 0, 0, tiled=True
    )

    wide_cols = 2 * per * SPAN
    field = call(
        functools.partial(update_kernel, per),
        jax.ShapeDtypeStruct((leaves, SPAN, wide_cols), BF16),
        in_specs=[scalar, whole, hbm],
        scratch_shapes=[pltpu.VMEM(tab.shape, BF16), dma((1,))],
    )(core.reshape(1), got, tab)
    summed, field = lax.optimization_barrier((summed, field))
    field = lax.all_to_all(field, "leaf", 0, 0, tiled=True)
    field = jnp.broadcast_to(field[None], (NX,) + field.shape)
    mine = lax.all_to_all(field, "x", 0, 0, tiled=True)
    step = 3
    residual = call(
        functools.partial(residual_kernel, step),
        jax.ShapeDtypeStruct((SPAN, own_cols), F32),
        grid=(rows // step,),
        in_specs=[
            pl.BlockSpec((SPAN, step * QUAD), lambda i: (0, i)),
            pl.BlockSpec((SPAN, step * QUAD), lambda i: (0, i)),
            pl.BlockSpec((1, 16, LANES), lambda i: (0, 0, 0)),
            whole,
            whole,
        ],
        out_specs=pl.BlockSpec((SPAN, step * QUAD), lambda i: (0, i)),
        cost_estimate=pl.CostEstimate(flops=10**9, bytes_accessed=16 * 10**6, transcendentals=0),
    )(summed, m, own_ids, wide, ct)

    residual, mine = lax.optimization_barrier((residual, mine))
    other = lax.ppermute(mine, "core", [(0, 1), (1, 0)])

    def place(who, piece, base):
        more = {} if base is None else {"input_output_aliases": {2: 0}}
        operands = (who.reshape(1), piece) + (() if base is None else (base,))
        return call(
            place_kernel if base is not None else functools.partial(place_first, place_kernel),
            jax.ShapeDtypeStruct((SPAN, columns), BF16),
            in_specs=[scalar] + [anywhere] * (len(operands) - 1),
            out_specs=hbm,
            scratch_shapes=[dma((NX * leaves,))],
            cost_estimate=pl.CostEstimate(flops=0, bytes_accessed=4 * 10**6, transcendentals=0),
            **more,
        )(*operands)

    update = place(core, mine, None)
    update = place(1 - core, other, update)
    return (residual[None], update)


def solution(mesh):
    reps, leaves = mesh.devices.shape
    nz = reps // (NX * NC)
    fine = Mesh(mesh.devices.reshape(NX, nz, NC, leaves), ("x", "z", "core", "leaf"))
    rep = ("x", "z", "core")
    placed = (
        P(rep, "leaf", None, None),
        P(rep, None, "leaf"),
        P(rep, None, "leaf", None),
        P(rep, None, "leaf"),
    )
    return jax.shard_map(
        functools.partial(on_device, nz, leaves),
        mesh=fine,
        in_specs=placed,
        out_specs=(P(rep, None, "leaf"), P()),
        check_vma=False,
    )
```

```python
import functools

import jax
import jax.numpy as jnp
import numpy as np
from jax import lax
from jax.experimental import pallas as pl
from jax.experimental.pallas import tpu as pltpu
from jax.sharding import Mesh, PartitionSpec as P

SPAN = 64
LANES = 128
QUAD = 4 * SPAN
NX, NC = 4, 2
F32, BF16 = jnp.float32, jnp.bfloat16
VMEM_LIMIT = 24 * 1024 * 1024


def split(a):
    hi = a.astype(BF16)
    return hi, (a - hi.astype(F32)).astype(BF16)


def tables():
    f = np.arange(SPAN)[:, None]
    i = np.arange(SPAN)[None, :]
    scale = np.where(f == 0, np.sqrt(1.0 / SPAN), np.sqrt(2.0 / SPAN))
    c = (scale * np.cos(np.pi * (2 * i + 1) * f / (2 * SPAN))).astype(np.float32)
    return c


def two_parts(c):
    hi = c.astype(jnp.bfloat16)
    lo = (c - hi.astype(np.float32)).astype(jnp.bfloat16)
    return hi, lo


def dot(a, b):
    return lax.dot_general(a, b, (((1,), (0,)), ((), ())), preferred_element_type=F32)


def dot_t(a, b):
    return lax.dot_general(a, b, (((1,), (1,)), ((), ())), preferred_element_type=F32)


def quads(x):
    n = x.shape[1] // QUAD
    return jnp.concatenate([x[:, QUAD * a : QUAD * (a + 1)] for a in range(n)], axis=0)


def lane_iota(shape):
    return lax.broadcasted_iota(jnp.int32, shape, len(shape) - 1)


def column_transform(x32, wide, hi_only):
    hi, lo = split(x32)
    both = dot(hi, wide)
    return both[:, :QUAD] + both[:, QUAD:] + dot(lo, hi_only)


def frequencies(ids):
    known = jnp.maximum(ids, 0)
    return lax.shift_right_logical(known, 6), jnp.bitwise_and(known, SPAN - 1)


def picked(f, ids, rows):
    lane = lane_iota((SPAN, LANES))
    _, v = frequencies(ids)
    at = jnp.broadcast_to(v, (SPAN, LANES)) + jnp.bitwise_and(lax.shift_left(lane, 1), SPAN)
    left = jnp.take_along_axis(f[:, :LANES], at, axis=1, mode="promise_in_bounds")
    right = jnp.take_along_axis(f[:, LANES:], at, axis=1, mode="promise_in_bounds")
    value = jnp.sum(jnp.where(lane < SPAN, left, right) * rows, axis=0, keepdims=True)
    return jnp.where(ids >= 0, value, 0.0)


def fetch(pairs, sems):
    copies = [pltpu.make_async_copy(src, dst, sems.at[i]) for i, (src, dst) in enumerate(pairs)]
    for copy in copies:
        copy.start()
    return copies


def ids_kernel(picks_hbm, counts_hbm, out_ref, picks_ref, counts_ref, sems):
    for copy in fetch([(picks_hbm, picks_ref), (counts_hbm, counts_ref)], sems):
        copy.wait()
    slots, n = picks_ref.shape
    slot = lax.broadcasted_iota(jnp.int32, (slots, n), 0)
    ids = jnp.where(slot < counts_ref[...], picks_ref[...], -1).T
    rows = n // 4
    lines = [
        jnp.concatenate([ids[4 * a + g : 4 * a + g + 1, :] for g in range(4)], axis=1)
        for a in range(rows)
    ]
    lines.append(jnp.full((out_ref.shape[1] - rows, LANES), -1, jnp.int32))
    full = jnp.concatenate(lines, axis=0)
    for y in range(out_ref.shape[0]):
        out_ref[y] = full


def dense_kernel(
    leaves, me_ref, g_hbm, m_hbm, wide_hbm, f_hbm, buf, m_ref, wide_ref, f_ref, sems, outs
):
    cols = g_hbm.shape[1] // leaves
    pairs = [(wide_hbm, wide_ref)]
    pairs += [(g_hbm.at[:, y * cols : (y + 1) * cols], buf.at[y]) for y in range(leaves)]
    pairs += [(m_hbm, m_ref)]
    copies = fetch(pairs, sems)
    copies[0].wait()
    me = me_ref[0]
    back = []
    for y in range(leaves):
        copies[1 + y].wait()
        both = dot(quads(buf[y]), wide_ref[...])
        f_ref[y] = both[:, :QUAD] + both[:, QUAD:]
        if y == 0:
            copies[leaves + 1].wait()

        @pl.when(me == y)
        def _():
            own = column_transform(quads(0.9 * m_ref[...]), wide_ref[...], wide_ref[:, :QUAD])
            f_ref[y] += own

        copy = pltpu.make_async_copy(f_ref.at[y], f_hbm.at[y], outs.at[y])
        copy.start()
        back.append(copy)
    for copy in back:
        copy.wait()


def coeff_kernel(rows, f_hbm, ids_hbm, tab_hbm, out_ref, f_ref, ids_ref, tab_ref, sems):
    leaves = f_hbm.shape[0]
    pairs = [(ids_hbm, ids_ref), (tab_hbm, tab_ref)]
    first, second, *copies = fetch(pairs + [(f_hbm.at[y], f_ref.at[y]) for y in range(leaves)], sems)
    first.wait()
    second.wait()
    both = jnp.concatenate([tab_ref[2], tab_ref[3]], axis=0)
    short = lax.broadcasted_iota(jnp.int32, (SPAN, LANES), 0)
    for y in range(leaves):
        lines = [ids_ref[y, a : a + 1, :] for a in range(rows)]
        hot = [jnp.where(short == frequencies(ids)[0], 1.0, 0.0).astype(BF16) for ids in lines]
        table = dot(both, jnp.concatenate(hot, axis=1))
        table = table[:SPAN] + table[SPAN:]
        copies[y].wait()
        for a in range(rows):
            f = f_ref[y, SPAN * a : SPAN * (a + 1), :]
            out_ref[y, a : a + 1, :] = picked(f, lines[a], table[:, LANES * a : LANES * (a + 1)])
        out_ref[y, rows:, :] = jnp.zeros((out_ref.shape[1] - rows, LANES), F32)


def regroup_kernel(per, got_ref, ids_ref, out_ref):
    total = got_ref[0]
    for l in range(1, got_ref.shape[0]):
        total = total + got_ref[l]
    total = total.astype(BF16).astype(F32)
    ids = jnp.maximum(ids_ref[0], 0).astype(F32)
    low = lane_iota((1, LANES)) < SPAN
    for x in range(NX):
        for c in range(NC):
            keep = low if c == 0 else jnp.logical_not(low)
            full, half = per * x + (per - 1) * c, per * x + 1
            lines = []
            for of in (total, ids):
                lines += [of[full : full + 1], jnp.where(keep, of[half : half + 1], 0.0)]
            page = jnp.concatenate(lines, axis=0)
            for z in range(out_ref.shape[1]):
                out_ref[x, z, c] = page


def update_kernel(per, core_ref, got_ref, tab_hbm, out_ref, tab_ref, sems):
    (copy,) = fetch([(tab_hbm, tab_ref)], sems)
    peers = got_ref.shape[0]
    tall = lax.broadcasted_iota(jnp.int32, (2 * SPAN, LANES), 0)
    short = lax.broadcasted_iota(jnp.int32, (SPAN, LANES), 0)
    block = lax.shift_left(jnp.bitwise_and(lax.shift_right_logical(lane_iota((1, LANES)), 5), 1), 6)
    low = lane_iota((2, LANES)) < SPAN

    def two_peers(n):
        a, b = got_ref[n], got_ref[n + 1]
        turned_a, turned_b = pltpu.roll(a, SPAN, 1), pltpu.roll(b, SPAN, 1)
        pick = [jnp.concatenate([v[0:1], v[2:3]], axis=0) for v in (a, turned_a, b, turned_b)]
        first = jnp.where(low, pick[0], pick[3])
        second = jnp.where(low, pick[1], pick[2])
        third = jnp.concatenate([a[1:2] + turned_b[1:2], a[3:4] + turned_b[3:4]], axis=0)
        return first, second, third

    def four_peers(n, sums):
        pairs = [two_peers(4 * n), two_peers(4 * n + 2)]
        new = []
        for a in range(per):
            left, right = [], []
            for lines in pairs:
                value, ids = lines[a][0:1], lines[a][1:2].astype(jnp.int32)
                u = lax.shift_right_logical(ids, 6) + block
                v = jnp.bitwise_and(ids, SPAN - 1)
                left.append(jnp.where(tall == u, value, 0.0).astype(BF16))
                right.append(jnp.where(short == v, 1.0, 0.0).astype(BF16))
            new.append(
                sums[a] + dot_t(jnp.concatenate(left, axis=1), jnp.concatenate(right, axis=1))
            )
        return tuple(new)

    zero = jnp.zeros((2 * SPAN, SPAN), F32)
    sums = lax.fori_loop(0, peers // 4, four_peers, (zero,) * per, unroll=True)
    z = jnp.concatenate(sums, axis=0)
    z_hi, z_lo = split(z)
    copy.wait()
    c_hi, c_lo, ct_hi, ct_lo = [tab_ref[i] for i in range(4)]
    w = dot(z_hi, c_hi) + (dot(z_hi, c_lo) + dot(z_lo, c_hi))
    flat = jnp.concatenate([w[SPAN * b : SPAN * (b + 1)] for b in range(2 * per)], axis=1)
    w_hi, w_lo = split(flat)
    field = dot(ct_hi, w_hi) + (dot(ct_lo, w_hi) + dot(ct_hi, w_lo))
    edge = 2 * LANES
    turned = jnp.concatenate([field[:, edge:], field[:, :edge]], axis=1)
    field = jnp.where(core_ref[0] == 0, field, turned).astype(BF16)
    for y in range(out_ref.shape[0]):
        out_ref[y] = field


def residual_kernel(step, sum_ref, m_ref, ids_ref, wide_ref, ct_ref, out_ref):
    first = pl.program_id(0) * step
    x = 0.9 * m_ref[...] + sum_ref[...].astype(F32)
    f = column_transform(quads(x), wide_ref[...], wide_ref[:, :QUAD])
    ct = ct_ref[...]
    group = lax.shift_right_logical(lane_iota((SPAN, LANES)), 5)
    for a in range(step):
        ids = ids_ref[0, pl.ds(first + a, 1), :]
        u, v = [jnp.broadcast_to(w, (SPAN, LANES)) for w in frequencies(ids)]
        rows = jnp.take_along_axis(ct, u, axis=1, mode="promise_in_bounds")
        cols = jnp.take_along_axis(ct, v, axis=1, mode="promise_in_bounds")
        value = picked(f[SPAN * a : SPAN * (a + 1)], ids, rows)
        cols = jnp.concatenate([jnp.where(group == b, cols, 0.0) for b in range(4)], axis=0)
        l_hi, l_lo = split(rows * value)
        r_hi, r_lo = split(cols)
        taken = dot_t(l_hi, r_hi) + (dot_t(l_hi, r_lo) + dot_t(l_lo, r_hi))
        out_ref[:, QUAD * a : QUAD * (a + 1)] = x[:, QUAD * a : QUAD * (a + 1)] - taken


def place_kernel(own, others, x_ref, core_ref, *refs):
    pieces, out_hbm, sem = refs[: len(own + others)], refs[-2], refs[-1]
    x, core = x_ref[0], core_ref[0]
    at = [jnp.bitwise_and(x + (NX - hops), NX - 1) * NC + core for hops in own]
    at += [jnp.bitwise_and(x + (NX - hops), NX - 1) * NC + (1 - core) for hops in others]
    leaves, _, cols = pieces[0].shape
    copies = []
    for i, piece in enumerate(pieces):
        for y in range(leaves):
            to = pl.multiple_of((y * NX * NC + at[i]) * cols, LANES)
            copies.append(
                pltpu.make_async_copy(piece.at[y], out_hbm.at[:, pl.ds(to, cols)], sem.at[len(copies)])
            )
    for copy in copies:
        copy.start()
    for copy in copies:
        copy.wait()


def call(kernel, out_shape, vmem=VMEM_LIMIT, **kw):
    return pl.pallas_call(
        kernel,
        out_shape=out_shape,
        compiler_params=pltpu.CompilerParams(vmem_limit_bytes=vmem),
        **kw,
    )


def on_device(nz, leaves, grads, momentum, picks, counts):
    c = tables()
    c_hi, c_lo = two_parts(c)
    ct_hi, ct_lo = two_parts(np.ascontiguousarray(c.T))
    eye = np.eye(4, dtype=np.float32)
    bd_hi = np.kron(eye, ct_hi.astype(np.float32)).astype(jnp.bfloat16)
    bd_lo = np.kron(eye, ct_lo.astype(np.float32)).astype(jnp.bfloat16)
    wide = jnp.asarray(np.concatenate([bd_hi, bd_lo], axis=1))
    tab = jnp.asarray(np.stack([c_hi, c_lo, ct_hi, ct_lo]))
    ct = jnp.asarray(np.concatenate([c.T, c.T], axis=1))

    columns = grads.shape[3]
    own_cols = columns // leaves
    blocks, slots = picks.shape[2:]
    rows = blocks // 4
    per = rows // NX
    peers = nz * NC
    g = grads.reshape(SPAN, columns)
    m = momentum.reshape(SPAN, own_cols)
    leaf = lax.axis_index("leaf")
    core = lax.axis_index("core")
    whole = pl.BlockSpec(memory_space=pltpu.VMEM)
    scalar = pl.BlockSpec(memory_space=pltpu.SMEM)
    hbm = pl.BlockSpec(memory_space=pltpu.HBM)
    anywhere = pl.BlockSpec(memory_space=pl.ANY)
    dma = pltpu.SemaphoreType.DMA

    summed = lax.psum_scatter(g, "leaf", scatter_dimension=1, tiled=True)

    own_ids = call(
        ids_kernel,
        jax.ShapeDtypeStruct((leaves, 16, LANES), jnp.int32),
        vmem=62 * 1024 * 1024,
        in_specs=[hbm, hbm],
        scratch_shapes=[
            pltpu.VMEM((slots, blocks), jnp.int32),
            pltpu.VMEM((1, blocks), jnp.int32),
            dma((2,)),
        ],
    )(picks.reshape(blocks, slots).T, counts.reshape(1, blocks))
    all_ids = lax.all_to_all(own_ids, "leaf", 0, 0, tiled=True)

    f = call(
        functools.partial(dense_kernel, leaves),
        jax.ShapeDtypeStruct((leaves, rows * SPAN, QUAD), F32),
        vmem=56 * 1024 * 1024,
        in_specs=[scalar, hbm, hbm, hbm],
        out_specs=hbm,
        scratch_shapes=[
            pltpu.VMEM((leaves, SPAN, own_cols), BF16),
            pltpu.VMEM((SPAN, own_cols), F32),
            pltpu.VMEM(wide.shape, BF16),
            pltpu.VMEM((leaves, rows * SPAN, QUAD), F32),
            dma((leaves + 2,)),
            dma((leaves,)),
        ],
        cost_estimate=pl.CostEstimate(flops=2 * 10**9, bytes_accessed=16 * 10**6, transcendentals=0),
    )(leaf.reshape(1), g, m, wide)

    partial = call(
        functools.partial(coeff_kernel, rows),
        jax.ShapeDtypeStruct((leaves, 16, LANES), F32),
        vmem=58 * 1024 * 1024,
        in_specs=[hbm, anywhere, hbm],
        scratch_shapes=[
            pltpu.VMEM((leaves, rows * SPAN, QUAD), F32),
            pltpu.VMEM(all_ids.shape, jnp.int32),
            pltpu.VMEM(tab.shape, BF16),
            dma((leaves + 2,)),
        ],
    )(f, all_ids, tab)
    got = lax.all_to_all(partial, "leaf", 0, 0, tiled=True)

    sent = call(
        functools.partial(regroup_kernel, per),
        jax.ShapeDtypeStruct((NX, nz, NC, 4, LANES), F32),
    )(got, own_ids)
    got = lax.all_to_all(
        sent.reshape(NX * peers, 4, LANES), ("x", "z", "core"), 0, 0, tiled=True
    )

    wide_cols = 2 * per * SPAN
    field = call(
        functools.partial(update_kernel, per),
        jax.ShapeDtypeStruct((leaves, SPAN, wide_cols), BF16),
        in_specs=[scalar, whole, hbm],
        scratch_shapes=[pltpu.VMEM(tab.shape, BF16), dma((1,))],
    )(core.reshape(1), got, tab)
    summed, field = lax.optimization_barrier((summed, field))
    field = lax.all_to_all(field, "leaf", 0, 0, tiled=True)

    def along_x(hops):
        return lax.ppermute(field, "x", [(i, (i + hops) % NX) for i in range(NX)])

    def across(a):
        return lax.ppermute(a, "core", [(0, 1), (1, 0)])

    mine = {0: field, 1: along_x(1), 3: along_x(3), 2: along_x(2)}

    step = 3
    residual = call(
        functools.partial(residual_kernel, step),
        jax.ShapeDtypeStruct((SPAN, own_cols), F32),
        grid=(rows // step,),
        in_specs=[
            pl.BlockSpec((SPAN, step * QUAD), lambda i: (0, i)),
            pl.BlockSpec((SPAN, step * QUAD), lambda i: (0, i)),
            pl.BlockSpec((1, 16, LANES), lambda i: (0, 0, 0)),
            whole,
            whole,
        ],
        out_specs=pl.BlockSpec((SPAN, step * QUAD), lambda i: (0, i)),
        cost_estimate=pl.CostEstimate(flops=10**9, bytes_accessed=16 * 10**6, transcendentals=0),
    )(summed, m, own_ids, wide, ct)

    residual, mine[2] = lax.optimization_barrier((residual, mine[2]))
    other = {hops: across(mine[hops]) for hops in (0, 1, 3, 2)}
    x = lax.axis_index("x")

    def place(own, others, base):
        pieces = [mine[hops] for hops in own] + [other[hops] for hops in others]
        last = () if base is None else (base,)
        return call(
            functools.partial(place_kernel, own, others),
            jax.ShapeDtypeStruct((SPAN, columns), BF16),
            in_specs=[scalar] * 2 + [anywhere] * (len(pieces) + len(last)),
            out_specs=hbm,
            scratch_shapes=[dma((len(pieces) * leaves,))],
            input_output_aliases={} if base is None else {len(pieces) + 2: 0},
            cost_estimate=pl.CostEstimate(flops=0, bytes_accessed=4 * 10**6, transcendentals=0),
        )(x.reshape(1), core.reshape(1), *pieces, *last)

    update = place((0, 1, 3), (0,), None)
    update = place((2,), (1, 3), update)
    update = place((), (2,), update)
    return (residual[None], update)


def solution(mesh):
    reps, leaves = mesh.devices.shape
    nz = reps // (NX * NC)
    fine = Mesh(mesh.devices.reshape(NX, nz, NC, leaves), ("x", "z", "core", "leaf"))
    rep = ("x", "z", "core")
    placed = (
        P(rep, "leaf", None, None),
        P(rep, None, "leaf"),
        P(rep, None, "leaf", None),
        P(rep, None, "leaf"),
    )
    return jax.shard_map(
        functools.partial(on_device, nz, leaves),
        mesh=fine,
        in_specs=placed,
        out_specs=(P(rep, None, "leaf"), P()),
        check_vma=False,
    )
```

```python
import functools

import jax
import jax.numpy as jnp
import numpy as np
from jax import lax
from jax.experimental import pallas as pl
from jax.experimental.pallas import tpu as pltpu
from jax.sharding import Mesh, PartitionSpec as P

SPAN = 64
LANES = 128
QUAD = 4 * SPAN
NX, NC = 4, 2
F32, BF16 = jnp.float32, jnp.bfloat16
VMEM_LIMIT = 24 * 1024 * 1024


def split(a):
    hi = a.astype(BF16)
    return hi, (a - hi.astype(F32)).astype(BF16)


def tables():
    f = np.arange(SPAN)[:, None]
    i = np.arange(SPAN)[None, :]
    scale = np.where(f == 0, np.sqrt(1.0 / SPAN), np.sqrt(2.0 / SPAN))
    c = (scale * np.cos(np.pi * (2 * i + 1) * f / (2 * SPAN))).astype(np.float32)
    return c


def two_parts(c):
    hi = c.astype(jnp.bfloat16)
    lo = (c - hi.astype(np.float32)).astype(jnp.bfloat16)
    return hi, lo


def dot(a, b):
    return lax.dot_general(a, b, (((1,), (0,)), ((), ())), preferred_element_type=F32)


def dot_t(a, b):
    return lax.dot_general(a, b, (((1,), (1,)), ((), ())), preferred_element_type=F32)


def quads(x):
    n = x.shape[1] // QUAD
    return jnp.concatenate([x[:, QUAD * a : QUAD * (a + 1)] for a in range(n)], axis=0)


def lane_iota(shape):
    return lax.broadcasted_iota(jnp.int32, shape, len(shape) - 1)


def column_transform(x32, wide, hi_only):
    hi, lo = split(x32)
    both = dot(hi, wide)
    return both[:, :QUAD] + both[:, QUAD:] + dot(lo, hi_only)


def frequencies(ids):
    known = jnp.maximum(ids, 0)
    return lax.shift_right_logical(known, 6), jnp.bitwise_and(known, SPAN - 1)


def picked(f, ids, rows):
    lane = lane_iota((SPAN, LANES))
    _, v = frequencies(ids)
    at = jnp.broadcast_to(v, (SPAN, LANES)) + jnp.bitwise_and(lax.shift_left(lane, 1), SPAN)
    left = jnp.take_along_axis(f[:, :LANES], at, axis=1, mode="promise_in_bounds")
    right = jnp.take_along_axis(f[:, LANES:], at, axis=1, mode="promise_in_bounds")
    value = jnp.sum(jnp.where(lane < SPAN, left, right) * rows, axis=0, keepdims=True)
    return jnp.where(ids >= 0, value, 0.0)


def fetch(pairs, sems):
    copies = [pltpu.make_async_copy(src, dst, sems.at[i]) for i, (src, dst) in enumerate(pairs)]
    for copy in copies:
        copy.start()
    return copies


def ids_kernel(picks_hbm, counts_hbm, out_ref, picks_ref, counts_ref, sems):
    for copy in fetch([(picks_hbm, picks_ref), (counts_hbm, counts_ref)], sems):
        copy.wait()
    slots, n = picks_ref.shape
    slot = lax.broadcasted_iota(jnp.int32, (slots, n), 0)
    ids = jnp.where(slot < counts_ref[...], picks_ref[...], -1).T
    rows = n // 4
    lines = [
        jnp.concatenate([ids[4 * a + g : 4 * a + g + 1, :] for g in range(4)], axis=1)
        for a in range(rows)
    ]
    lines.append(jnp.full((out_ref.shape[1] - rows, LANES), -1, jnp.int32))
    full = jnp.concatenate(lines, axis=0)
    for y in range(out_ref.shape[0]):
        out_ref[y] = full


def dense_kernel(
    leaves, me_ref, g_hbm, m_hbm, wide_hbm, f_hbm, buf, m_ref, wide_ref, f_ref, sems, outs
):
    cols = g_hbm.shape[1] // leaves
    pairs = [(wide_hbm, wide_ref)]
    pairs += [(g_hbm.at[:, y * cols : (y + 1) * cols], buf.at[y]) for y in range(leaves)]
    pairs += [(m_hbm, m_ref)]
    copies = fetch(pairs, sems)
    copies[0].wait()
    me = me_ref[0]
    back = []
    for y in range(leaves):
        copies[1 + y].wait()
        both = dot(quads(buf[y]), wide_ref[...])
        f_ref[y] = both[:, :QUAD] + both[:, QUAD:]
        if y == 0:
            copies[leaves + 1].wait()

        @pl.when(me == y)
        def _():
            own = column_transform(quads(0.9 * m_ref[...]), wide_ref[...], wide_ref[:, :QUAD])
            f_ref[y] += own

        copy = pltpu.make_async_copy(f_ref.at[y], f_hbm.at[y], outs.at[y])
        copy.start()
        back.append(copy)
    for copy in back:
        copy.wait()


def coeff_kernel(rows, f_hbm, ids_hbm, tab_hbm, out_ref, f_ref, ids_ref, tab_ref, sems):
    leaves = f_hbm.shape[0]
    pairs = [(ids_hbm, ids_ref), (tab_hbm, tab_ref)]
    first, second, *copies = fetch(pairs + [(f_hbm.at[y], f_ref.at[y]) for y in range(leaves)], sems)
    first.wait()
    second.wait()
    both = jnp.concatenate([tab_ref[2], tab_ref[3]], axis=0)
    short = lax.broadcasted_iota(jnp.int32, (SPAN, LANES), 0)
    for y in range(leaves):
        lines = [ids_ref[y, a : a + 1, :] for a in range(rows)]
        hot = [jnp.where(short == frequencies(ids)[0], 1.0, 0.0).astype(BF16) for ids in lines]
        table = dot(both, jnp.concatenate(hot, axis=1))
        table = table[:SPAN] + table[SPAN:]
        copies[y].wait()
        for a in range(rows):
            f = f_ref[y, SPAN * a : SPAN * (a + 1), :]
            out_ref[y, a : a + 1, :] = picked(f, lines[a], table[:, LANES * a : LANES * (a + 1)])
        out_ref[y, rows:, :] = jnp.zeros((out_ref.shape[1] - rows, LANES), F32)


def regroup_kernel(per, got_ref, ids_ref, out_ref):
    total = got_ref[0]
    for l in range(1, got_ref.shape[0]):
        total = total + got_ref[l]
    total = total.astype(BF16).astype(F32)
    ids = jnp.maximum(ids_ref[0], 0).astype(F32)
    low = lane_iota((1, LANES)) < SPAN
    for x in range(NX):
        for c in range(NC):
            keep = low if c == 0 else jnp.logical_not(low)
            full, half = per * x + (per - 1) * c, per * x + 1
            lines = []
            for of in (total, ids):
                lines += [of[full : full + 1], jnp.where(keep, of[half : half + 1], 0.0)]
            page = jnp.concatenate(lines, axis=0)
            for z in range(out_ref.shape[1]):
                out_ref[x, z, c] = page


def update_kernel(per, core_ref, got_ref, tab_hbm, out_ref, tab_ref, sems):
    (copy,) = fetch([(tab_hbm, tab_ref)], sems)
    peers = got_ref.shape[0]
    tall = lax.broadcasted_iota(jnp.int32, (2 * SPAN, LANES), 0)
    short = lax.broadcasted_iota(jnp.int32, (SPAN, LANES), 0)
    block = lax.shift_left(jnp.bitwise_and(lax.shift_right_logical(lane_iota((1, LANES)), 5), 1), 6)
    low = lane_iota((2, LANES)) < SPAN

    def two_peers(n):
        a, b = got_ref[n], got_ref[n + 1]
        turned_a, turned_b = pltpu.roll(a, SPAN, 1), pltpu.roll(b, SPAN, 1)
        pick = [jnp.concatenate([v[0:1], v[2:3]], axis=0) for v in (a, turned_a, b, turned_b)]
        first = jnp.where(low, pick[0], pick[3])
        second = jnp.where(low, pick[1], pick[2])
        third = jnp.concatenate([a[1:2] + turned_b[1:2], a[3:4] + turned_b[3:4]], axis=0)
        return first, second, third

    def four_peers(n, sums):
        pairs = [two_peers(4 * n), two_peers(4 * n + 2)]
        new = []
        for a in range(per):
            left, right = [], []
            for lines in pairs:
                value, ids = lines[a][0:1], lines[a][1:2].astype(jnp.int32)
                u = lax.shift_right_logical(ids, 6) + block
                v = jnp.bitwise_and(ids, SPAN - 1)
                left.append(jnp.where(tall == u, value, 0.0).astype(BF16))
                right.append(jnp.where(short == v, 1.0, 0.0).astype(BF16))
            new.append(
                sums[a] + dot_t(jnp.concatenate(left, axis=1), jnp.concatenate(right, axis=1))
            )
        return tuple(new)

    zero = jnp.zeros((2 * SPAN, SPAN), F32)
    sums = lax.fori_loop(0, peers // 4, four_peers, (zero,) * per, unroll=True)
    z = jnp.concatenate(sums, axis=0)
    z_hi, z_lo = split(z)
    copy.wait()
    c_hi, c_lo, ct_hi, ct_lo = [tab_ref[i] for i in range(4)]
    w = dot(z_hi, c_hi) + (dot(z_hi, c_lo) + dot(z_lo, c_hi))
    flat = jnp.concatenate([w[SPAN * b : SPAN * (b + 1)] for b in range(2 * per)], axis=1)
    w_hi, w_lo = split(flat)
    field = dot(ct_hi, w_hi) + (dot(ct_lo, w_hi) + dot(ct_hi, w_lo))
    edge = 2 * LANES
    turned = jnp.concatenate([field[:, edge:], field[:, :edge]], axis=1)
    field = jnp.where(core_ref[0] == 0, field, turned).astype(BF16)
    for y in range(out_ref.shape[0]):
        out_ref[y] = field


def residual_kernel(step, sum_ref, m_ref, ids_ref, wide_ref, ct_ref, out_ref):
    first = pl.program_id(0) * step
    x = 0.9 * m_ref[...] + sum_ref[...].astype(F32)
    f = column_transform(quads(x), wide_ref[...], wide_ref[:, :QUAD])
    ct = ct_ref[...]
    group = lax.shift_right_logical(lane_iota((SPAN, LANES)), 5)
    for a in range(step):
        ids = ids_ref[0, pl.ds(first + a, 1), :]
        u, v = [jnp.broadcast_to(w, (SPAN, LANES)) for w in frequencies(ids)]
        rows = jnp.take_along_axis(ct, u, axis=1, mode="promise_in_bounds")
        cols = jnp.take_along_axis(ct, v, axis=1, mode="promise_in_bounds")
        value = picked(f[SPAN * a : SPAN * (a + 1)], ids, rows)
        cols = jnp.concatenate([jnp.where(group == b, cols, 0.0) for b in range(4)], axis=0)
        l_hi, l_lo = split(rows * value)
        r_hi, r_lo = split(cols)
        taken = dot_t(l_hi, r_hi) + (dot_t(l_hi, r_lo) + dot_t(l_lo, r_hi))
        out_ref[:, QUAD * a : QUAD * (a + 1)] = x[:, QUAD * a : QUAD * (a + 1)] - taken


def place_kernel(own, others, x_ref, core_ref, *refs):
    out_hbm, sem = refs[-2], refs[-1]
    x, core = x_ref[0], core_ref[0]
    pieces, at = [], []
    for hops, c, ref in zip(own + others, [core] * len(own) + [1 - core] * len(others), refs):
        several = hops if isinstance(hops, tuple) else (hops,)
        pieces += [ref.at[i] for i in range(len(several))] if hops is several else [ref]
        at += [jnp.bitwise_and(x + (NX - n), NX - 1) * NC + c for n in several]
    leaves, _, cols = pieces[0].shape
    copies = []
    for i, piece in enumerate(pieces):
        for y in range(leaves):
            to = pl.multiple_of((y * NX * NC + at[i]) * cols, LANES)
            copies.append(
                pltpu.make_async_copy(piece.at[y], out_hbm.at[:, pl.ds(to, cols)], sem.at[len(copies)])
            )
    for copy in copies:
        copy.start()
    for copy in copies:
        copy.wait()


def call(kernel, out_shape, vmem=VMEM_LIMIT, **kw):
    return pl.pallas_call(
        kernel,
        out_shape=out_shape,
        compiler_params=pltpu.CompilerParams(vmem_limit_bytes=vmem),
        **kw,
    )


def on_device(nz, leaves, grads, momentum, picks, counts):
    c = tables()
    c_hi, c_lo = two_parts(c)
    ct_hi, ct_lo = two_parts(np.ascontiguousarray(c.T))
    eye = np.eye(4, dtype=np.float32)
    bd_hi = np.kron(eye, ct_hi.astype(np.float32)).astype(jnp.bfloat16)
    bd_lo = np.kron(eye, ct_lo.astype(np.float32)).astype(jnp.bfloat16)
    wide = jnp.asarray(np.concatenate([bd_hi, bd_lo], axis=1))
    tab = jnp.asarray(np.stack([c_hi, c_lo, ct_hi, ct_lo]))
    ct = jnp.asarray(np.concatenate([c.T, c.T], axis=1))

    columns = grads.shape[3]
    own_cols = columns // leaves
    blocks, slots = picks.shape[2:]
    rows = blocks // 4
    per = rows // NX
    peers = nz * NC
    g = grads.reshape(SPAN, columns)
    m = momentum.reshape(SPAN, own_cols)
    leaf = lax.axis_index("leaf")
    core = lax.axis_index("core")
    whole = pl.BlockSpec(memory_space=pltpu.VMEM)
    scalar = pl.BlockSpec(memory_space=pltpu.SMEM)
    hbm = pl.BlockSpec(memory_space=pltpu.HBM)
    anywhere = pl.BlockSpec(memory_space=pl.ANY)
    dma = pltpu.SemaphoreType.DMA

    summed = lax.psum_scatter(g, "leaf", scatter_dimension=1, tiled=True)

    own_ids = call(
        ids_kernel,
        jax.ShapeDtypeStruct((leaves, 16, LANES), jnp.int32),
        vmem=62 * 1024 * 1024,
        in_specs=[hbm, hbm],
        scratch_shapes=[
            pltpu.VMEM((slots, blocks), jnp.int32),
            pltpu.VMEM((1, blocks), jnp.int32),
            dma((2,)),
        ],
    )(picks.reshape(blocks, slots).T, counts.reshape(1, blocks))
    all_ids = lax.all_to_all(own_ids, "leaf", 0, 0, tiled=True)

    f = call(
        functools.partial(dense_kernel, leaves),
        jax.ShapeDtypeStruct((leaves, rows * SPAN, QUAD), F32),
        vmem=56 * 1024 * 1024,
        in_specs=[scalar, hbm, hbm, hbm],
        out_specs=hbm,
        scratch_shapes=[
            pltpu.VMEM((leaves, SPAN, own_cols), BF16),
            pltpu.VMEM((SPAN, own_cols), F32),
            pltpu.VMEM(wide.shape, BF16),
            pltpu.VMEM((leaves, rows * SPAN, QUAD), F32),
            dma((leaves + 2,)),
            dma((leaves,)),
        ],
        cost_estimate=pl.CostEstimate(flops=2 * 10**9, bytes_accessed=16 * 10**6, transcendentals=0),
    )(leaf.reshape(1), g, m, wide)

    partial = call(
        functools.partial(coeff_kernel, rows),
        jax.ShapeDtypeStruct((leaves, 16, LANES), F32),
        vmem=50 * 1024 * 1024,
        in_specs=[hbm, anywhere, hbm],
        scratch_shapes=[
            pltpu.VMEM((leaves, rows * SPAN, QUAD), F32),
            pltpu.VMEM(all_ids.shape, jnp.int32),
            pltpu.VMEM(tab.shape, BF16),
            dma((leaves + 2,)),
        ],
    )(f, all_ids, tab)
    got = lax.all_to_all(partial, "leaf", 0, 0, tiled=True)

    sent = call(
        functools.partial(regroup_kernel, per),
        jax.ShapeDtypeStruct((NX, nz, NC, 4, LANES), F32),
    )(got, own_ids)
    got = lax.all_to_all(
        sent.reshape(NX * peers, 4, LANES), ("x", "z", "core"), 0, 0, tiled=True
    )

    wide_cols = 2 * per * SPAN
    field = call(
        functools.partial(update_kernel, per),
        jax.ShapeDtypeStruct((leaves, SPAN, wide_cols), BF16),
        in_specs=[scalar, whole, hbm],
        scratch_shapes=[pltpu.VMEM(tab.shape, BF16), dma((1,))],
    )(core.reshape(1), got, tab)
    summed, field = lax.optimization_barrier((summed, field))
    field = lax.all_to_all(field, "leaf", 0, 0, tiled=True)

    def along_x(hops):
        return lax.ppermute(field, "x", [(i, (i + hops) % NX) for i in range(NX)])

    def across(a):
        return lax.ppermute(a, "core", [(0, 1), (1, 0)])

    mine = {hops: along_x(hops) for hops in (2, 1, 3)}

    step = 3
    residual = call(
        functools.partial(residual_kernel, step),
        jax.ShapeDtypeStruct((SPAN, own_cols), F32),
        grid=(rows // step,),
        in_specs=[
            pl.BlockSpec((SPAN, step * QUAD), lambda i: (0, i)),
            pl.BlockSpec((SPAN, step * QUAD), lambda i: (0, i)),
            pl.BlockSpec((1, 16, LANES), lambda i: (0, 0, 0)),
            whole,
            whole,
        ],
        out_specs=pl.BlockSpec((SPAN, step * QUAD), lambda i: (0, i)),
        cost_estimate=pl.CostEstimate(flops=10**9, bytes_accessed=16 * 10**6, transcendentals=0),
    )(summed, m, own_ids, wide, ct)

    beside = across(field)
    order = (1, 3, 2)
    rest = jnp.stack([mine[hops] for hops in order])
    residual, beside, rest = lax.optimization_barrier((residual, beside, rest))
    x = lax.axis_index("x")

    def place(own, others, base):
        pieces = [*own.values(), *others.values()]
        last = () if base is None else (base,)
        return call(
            functools.partial(place_kernel, list(own), list(others)),
            jax.ShapeDtypeStruct((SPAN, columns), BF16),
            in_specs=[scalar] * 2 + [anywhere] * (len(pieces) + len(last)),
            out_specs=hbm,
            scratch_shapes=[dma((NX * NC * leaves,))],
            input_output_aliases={} if base is None else {len(pieces) + 2: 0},
            cost_estimate=pl.CostEstimate(flops=0, bytes_accessed=4 * 10**6, transcendentals=0),
        )(x.reshape(1), core.reshape(1), *pieces, *last)

    update = place({0: field, order: rest}, {0: beside}, None)
    update = place({}, {order: across(rest)}, update)
    return (residual[None], update)


def solution(mesh):
    reps, leaves = mesh.devices.shape
    nz = reps // (NX * NC)
    fine = Mesh(mesh.devices.reshape(NX, nz, NC, leaves), ("x", "z", "core", "leaf"))
    rep = ("x", "z", "core")
    placed = (
        P(rep, "leaf", None, None),
        P(rep, None, "leaf"),
        P(rep, None, "leaf", None),
        P(rep, None, "leaf"),
    )
    return jax.shard_map(
        functools.partial(on_device, nz, leaves),
        mesh=fine,
        in_specs=placed,
        out_specs=(P(rep, None, "leaf"), P()),
        check_vma=False,
    )
```

```python
import functools

import jax
import jax.numpy as jnp
import numpy as np
from jax import lax
from jax.experimental import pallas as pl
from jax.experimental.pallas import tpu as pltpu
from jax.sharding import Mesh, PartitionSpec as P

SPAN = 64
LANES = 128
QUAD = 4 * SPAN
NX, NC = 4, 2
F32, BF16 = jnp.float32, jnp.bfloat16
VMEM_LIMIT = 24 * 1024 * 1024


def split(a):
    hi = a.astype(BF16)
    return hi, (a - hi.astype(F32)).astype(BF16)


def tables():
    f = np.arange(SPAN)[:, None]
    i = np.arange(SPAN)[None, :]
    scale = np.where(f == 0, np.sqrt(1.0 / SPAN), np.sqrt(2.0 / SPAN))
    c = (scale * np.cos(np.pi * (2 * i + 1) * f / (2 * SPAN))).astype(np.float32)
    return c


def two_parts(c):
    hi = c.astype(jnp.bfloat16)
    lo = (c - hi.astype(np.float32)).astype(jnp.bfloat16)
    return hi, lo


def dot(a, b):
    return lax.dot_general(a, b, (((1,), (0,)), ((), ())), preferred_element_type=F32)


def dot_t(a, b):
    return lax.dot_general(a, b, (((1,), (1,)), ((), ())), preferred_element_type=F32)


def quads(x):
    n = x.shape[1] // QUAD
    return jnp.concatenate([x[:, QUAD * a : QUAD * (a + 1)] for a in range(n)], axis=0)


def lane_iota(shape):
    return lax.broadcasted_iota(jnp.int32, shape, len(shape) - 1)


def column_transform(x32, wide, hi_only):
    hi, lo = split(x32)
    both = dot(hi, wide)
    return both[:, :QUAD] + both[:, QUAD:] + dot(lo, hi_only)


def frequencies(ids):
    known = jnp.maximum(ids, 0)
    return lax.shift_right_logical(known, 6), jnp.bitwise_and(known, SPAN - 1)


def picked(f, ids, rows):
    lane = lane_iota((SPAN, LANES))
    _, v = frequencies(ids)
    at = jnp.broadcast_to(v, (SPAN, LANES)) + jnp.bitwise_and(lax.shift_left(lane, 1), SPAN)
    left = jnp.take_along_axis(f[:, :LANES], at, axis=1, mode="promise_in_bounds")
    right = jnp.take_along_axis(f[:, LANES:], at, axis=1, mode="promise_in_bounds")
    value = jnp.sum(jnp.where(lane < SPAN, left, right) * rows, axis=0, keepdims=True)
    return jnp.where(ids >= 0, value, 0.0)


def fetch(pairs, sems):
    copies = [pltpu.make_async_copy(src, dst, sems.at[i]) for i, (src, dst) in enumerate(pairs)]
    for copy in copies:
        copy.start()
    return copies


def ids_kernel(picks_hbm, counts_hbm, out_ref, picks_ref, counts_ref, sems):
    for copy in fetch([(picks_hbm, picks_ref), (counts_hbm, counts_ref)], sems):
        copy.wait()
    slots, n = picks_ref.shape
    slot = lax.broadcasted_iota(jnp.int32, (slots, n), 0)
    ids = jnp.where(slot < counts_ref[...], picks_ref[...], -1).T
    rows = n // 4
    lines = [
        jnp.concatenate([ids[4 * a + g : 4 * a + g + 1, :] for g in range(4)], axis=1)
        for a in range(rows)
    ]
    lines.append(jnp.full((out_ref.shape[1] - rows, LANES), -1, jnp.int32))
    full = jnp.concatenate(lines, axis=0)
    for y in range(out_ref.shape[0]):
        out_ref[y] = full


def dense_kernel(
    leaves, me_ref, g_hbm, m_hbm, wide_hbm, f_hbm, buf, m_ref, wide_ref, f_ref, sems, outs
):
    cols = g_hbm.shape[1] // leaves
    pairs = [(wide_hbm, wide_ref)]
    pairs += [(g_hbm.at[:, y * cols : (y + 1) * cols], buf.at[y]) for y in range(leaves)]
    pairs += [(m_hbm, m_ref)]
    copies = fetch(pairs, sems)
    copies[0].wait()
    me = me_ref[0]
    back = []
    for y in range(leaves):
        copies[1 + y].wait()
        both = dot(quads(buf[y]), wide_ref[...])
        f_ref[y] = both[:, :QUAD] + both[:, QUAD:]
        if y == 0:
            copies[leaves + 1].wait()

        @pl.when(me == y)
        def _():
            own = column_transform(quads(0.9 * m_ref[...]), wide_ref[...], wide_ref[:, :QUAD])
            f_ref[y] += own

        copy = pltpu.make_async_copy(f_ref.at[y], f_hbm.at[y], outs.at[y])
        copy.start()
        back.append(copy)
    for copy in back:
        copy.wait()


def coeff_kernel(rows, f_hbm, ids_hbm, tab_hbm, out_ref, f_ref, ids_ref, tab_ref, sems):
    leaves = f_hbm.shape[0]
    pairs = [(ids_hbm, ids_ref), (tab_hbm, tab_ref)]
    first, second, *copies = fetch(pairs + [(f_hbm.at[y], f_ref.at[y]) for y in range(leaves)], sems)
    first.wait()
    second.wait()
    both = jnp.concatenate([tab_ref[2], tab_ref[3]], axis=0)
    short = lax.broadcasted_iota(jnp.int32, (SPAN, LANES), 0)
    for y in range(leaves):
        lines = [ids_ref[y, a : a + 1, :] for a in range(rows)]
        hot = [jnp.where(short == frequencies(ids)[0], 1.0, 0.0).astype(BF16) for ids in lines]
        table = dot(both, jnp.concatenate(hot, axis=1))
        table = table[:SPAN] + table[SPAN:]
        copies[y].wait()
        for a in range(rows):
            f = f_ref[y, SPAN * a : SPAN * (a + 1), :]
            out_ref[y, a : a + 1, :] = picked(f, lines[a], table[:, LANES * a : LANES * (a + 1)])
        out_ref[y, rows:, :] = jnp.zeros((out_ref.shape[1] - rows, LANES), F32)


def regroup_kernel(per, got_ref, ids_ref, out_ref):
    total = got_ref[0]
    for l in range(1, got_ref.shape[0]):
        total = total + got_ref[l]
    total = total.astype(BF16).astype(F32)
    ids = jnp.maximum(ids_ref[0], 0).astype(F32)
    low = lane_iota((1, LANES)) < SPAN
    for x in range(NX):
        for c in range(NC):
            keep = low if c == 0 else jnp.logical_not(low)
            full, half = per * x + (per - 1) * c, per * x + 1
            value, index = total[half : half + 1], ids[half : half + 1]
            mixed = jnp.where(keep, value, pltpu.roll(index, SPAN, 1))
            page = jnp.concatenate([total[full : full + 1], mixed, ids[full : full + 1]], axis=1)
            for z in range(out_ref.shape[1]):
                out_ref[x, z, c] = page


def update_kernel(per, core_ref, got_ref, tab_hbm, out_ref, tab_ref, sems):
    (copy,) = fetch([(tab_hbm, tab_ref)], sems)
    peers = got_ref.shape[0]
    tall = lax.broadcasted_iota(jnp.int32, (2 * SPAN, LANES), 0)
    short = lax.broadcasted_iota(jnp.int32, (SPAN, LANES), 0)
    block = lax.shift_left(jnp.bitwise_and(lax.shift_right_logical(lane_iota((1, LANES)), 5), 1), 6)
    low = lane_iota((1, LANES)) < SPAN
    first_core = core_ref[0] == 0

    def two_peers(n):
        a, b = got_ref[n], got_ref[n + 1]
        mixed_a, mixed_b = a[:, LANES : 2 * LANES], b[:, LANES : 2 * LANES]
        turned_a, turned_b = pltpu.roll(mixed_a, SPAN, 1), pltpu.roll(mixed_b, SPAN, 1)
        firsts, seconds = [], []
        for at in (0, 2 * LANES):
            one, two = a[:, at : at + LANES], b[:, at : at + LANES]
            firsts.append(jnp.where(low, one, pltpu.roll(two, SPAN, 1)))
            seconds.append(jnp.where(low, pltpu.roll(one, SPAN, 1), two))
        here = jnp.where(low, mixed_a, turned_b)
        there = jnp.where(low, turned_a, mixed_b)
        value = jnp.where(first_core, here, there)
        index = jnp.where(first_core, there, here)
        return firsts, seconds, (value, index)

    def four_peers(n, sums):
        pairs = [two_peers(4 * n), two_peers(4 * n + 2)]
        new = []
        for a in range(per):
            left, right = [], []
            for lines in pairs:
                value, ids = lines[a][0], lines[a][1].astype(jnp.int32)
                u = lax.shift_right_logical(ids, 6) + block
                v = jnp.bitwise_and(ids, SPAN - 1)
                left.append(jnp.where(tall == u, value, 0.0).astype(BF16))
                right.append(jnp.where(short == v, 1.0, 0.0).astype(BF16))
            new.append(
                sums[a] + dot_t(jnp.concatenate(left, axis=1), jnp.concatenate(right, axis=1))
            )
        return tuple(new)

    zero = jnp.zeros((2 * SPAN, SPAN), F32)
    sums = lax.fori_loop(0, peers // 4, four_peers, (zero,) * per, unroll=True)
    z = jnp.concatenate(sums, axis=0)
    z_hi, z_lo = split(z)
    copy.wait()
    c_hi, c_lo, ct_hi, ct_lo = [tab_ref[i] for i in range(4)]
    w = dot(z_hi, c_hi) + (dot(z_hi, c_lo) + dot(z_lo, c_hi))
    flat = jnp.concatenate([w[SPAN * b : SPAN * (b + 1)] for b in range(2 * per)], axis=1)
    w_hi, w_lo = split(flat)
    field = dot(ct_hi, w_hi) + (dot(ct_lo, w_hi) + dot(ct_hi, w_lo))
    edge = 2 * LANES
    turned = jnp.concatenate([field[:, edge:], field[:, :edge]], axis=1)
    field = jnp.where(core_ref[0] == 0, field, turned).astype(BF16)
    for y in range(out_ref.shape[0]):
        out_ref[y] = field


def residual_kernel(step, sum_ref, m_ref, ids_ref, wide_ref, ct_ref, out_ref):
    first = pl.program_id(0) * step
    x = 0.9 * m_ref[...] + sum_ref[...].astype(F32)
    f = column_transform(quads(x), wide_ref[...], wide_ref[:, :QUAD])
    ct = ct_ref[...]
    group = lax.shift_right_logical(lane_iota((SPAN, LANES)), 5)
    for a in range(step):
        ids = ids_ref[0, pl.ds(first + a, 1), :]
        u, v = [jnp.broadcast_to(w, (SPAN, LANES)) for w in frequencies(ids)]
        rows = jnp.take_along_axis(ct, u, axis=1, mode="promise_in_bounds")
        cols = jnp.take_along_axis(ct, v, axis=1, mode="promise_in_bounds")
        value = picked(f[SPAN * a : SPAN * (a + 1)], ids, rows)
        cols = jnp.concatenate([jnp.where(group == b, cols, 0.0) for b in range(4)], axis=0)
        l_hi, l_lo = split(rows * value)
        r_hi, r_lo = split(cols)
        taken = dot_t(l_hi, r_hi) + (dot_t(l_hi, r_lo) + dot_t(l_lo, r_hi))
        out_ref[:, QUAD * a : QUAD * (a + 1)] = x[:, QUAD * a : QUAD * (a + 1)] - taken


def place_kernel(own, others, x_ref, core_ref, *refs):
    out_hbm, sem = refs[-2], refs[-1]
    x, core = x_ref[0], core_ref[0]
    pieces, at = [], []
    for hops, c, ref in zip(own + others, [core] * len(own) + [1 - core] * len(others), refs):
        several = hops if isinstance(hops, tuple) else (hops,)
        pieces += [ref.at[i] for i in range(len(several))] if hops is several else [ref]
        at += [jnp.bitwise_and(x + (NX - n), NX - 1) * NC + c for n in several]
    leaves, _, cols = pieces[0].shape
    copies = []
    for i, piece in enumerate(pieces):
        for y in range(leaves):
            to = pl.multiple_of((y * NX * NC + at[i]) * cols, LANES)
            copies.append(
                pltpu.make_async_copy(piece.at[y], out_hbm.at[:, pl.ds(to, cols)], sem.at[len(copies)])
            )
    for copy in copies:
        copy.start()
    for copy in copies:
        copy.wait()


def call(kernel, out_shape, vmem=VMEM_LIMIT, **kw):
    return pl.pallas_call(
        kernel,
        out_shape=out_shape,
        compiler_params=pltpu.CompilerParams(vmem_limit_bytes=vmem),
        **kw,
    )


def on_device(nz, leaves, grads, momentum, picks, counts):
    c = tables()
    c_hi, c_lo = two_parts(c)
    ct_hi, ct_lo = two_parts(np.ascontiguousarray(c.T))
    eye = np.eye(4, dtype=np.float32)
    bd_hi = np.kron(eye, ct_hi.astype(np.float32)).astype(jnp.bfloat16)
    bd_lo = np.kron(eye, ct_lo.astype(np.float32)).astype(jnp.bfloat16)
    wide = jnp.asarray(np.concatenate([bd_hi, bd_lo], axis=1))
    tab = jnp.asarray(np.stack([c_hi, c_lo, ct_hi, ct_lo]))
    ct = jnp.asarray(np.concatenate([c.T, c.T], axis=1))

    columns = grads.shape[3]
    own_cols = columns // leaves
    blocks, slots = picks.shape[2:]
    rows = blocks // 4
    per = rows // NX
    peers = nz * NC
    g = grads.reshape(SPAN, columns)
    m = momentum.reshape(SPAN, own_cols)
    leaf = lax.axis_index("leaf")
    core = lax.axis_index("core")
    whole = pl.BlockSpec(memory_space=pltpu.VMEM)
    scalar = pl.BlockSpec(memory_space=pltpu.SMEM)
    hbm = pl.BlockSpec(memory_space=pltpu.HBM)
    anywhere = pl.BlockSpec(memory_space=pl.ANY)
    dma = pltpu.SemaphoreType.DMA

    summed = lax.psum_scatter(g, "leaf", scatter_dimension=1, tiled=True)

    own_ids = call(
        ids_kernel,
        jax.ShapeDtypeStruct((leaves, 16, LANES), jnp.int32),
        vmem=62 * 1024 * 1024,
        in_specs=[hbm, hbm],
        scratch_shapes=[
            pltpu.VMEM((slots, blocks), jnp.int32),
            pltpu.VMEM((1, blocks), jnp.int32),
            dma((2,)),
        ],
    )(picks.reshape(blocks, slots).T, counts.reshape(1, blocks))
    all_ids = lax.all_to_all(own_ids, "leaf", 0, 0, tiled=True)

    f = call(
        functools.partial(dense_kernel, leaves),
        jax.ShapeDtypeStruct((leaves, rows * SPAN, QUAD), F32),
        vmem=56 * 1024 * 1024,
        in_specs=[scalar, hbm, hbm, hbm],
        out_specs=hbm,
        scratch_shapes=[
            pltpu.VMEM((leaves, SPAN, own_cols), BF16),
            pltpu.VMEM((SPAN, own_cols), F32),
            pltpu.VMEM(wide.shape, BF16),
            pltpu.VMEM((leaves, rows * SPAN, QUAD), F32),
            dma((leaves + 2,)),
            dma((leaves,)),
        ],
        cost_estimate=pl.CostEstimate(flops=2 * 10**9, bytes_accessed=16 * 10**6, transcendentals=0),
    )(leaf.reshape(1), g, m, wide)

    partial = call(
        functools.partial(coeff_kernel, rows),
        jax.ShapeDtypeStruct((leaves, 16, LANES), F32),
        vmem=50 * 1024 * 1024,
        in_specs=[hbm, anywhere, hbm],
        scratch_shapes=[
            pltpu.VMEM((leaves, rows * SPAN, QUAD), F32),
            pltpu.VMEM(all_ids.shape, jnp.int32),
            pltpu.VMEM(tab.shape, BF16),
            dma((leaves + 2,)),
        ],
    )(f, all_ids, tab)
    got = lax.all_to_all(partial, "leaf", 0, 0, tiled=True)

    sent = call(
        functools.partial(regroup_kernel, per),
        jax.ShapeDtypeStruct((NX, nz, NC, 1, 3 * LANES), F32),
    )(got, own_ids)
    got = lax.all_to_all(
        sent.reshape(NX * peers, 1, 3 * LANES), ("x", "z", "core"), 0, 0, tiled=True
    )

    wide_cols = 2 * per * SPAN
    field = call(
        functools.partial(update_kernel, per),
        jax.ShapeDtypeStruct((leaves, SPAN, wide_cols), BF16),
        in_specs=[scalar, whole, hbm],
        scratch_shapes=[pltpu.VMEM(tab.shape, BF16), dma((1,))],
    )(core.reshape(1), got, tab)
    summed, field = lax.optimization_barrier((summed, field))
    field = lax.all_to_all(field, "leaf", 0, 0, tiled=True)

    def along_x(hops):
        return lax.ppermute(field, "x", [(i, (i + hops) % NX) for i in range(NX)])

    def across(a):
        return lax.ppermute(a, "core", [(0, 1), (1, 0)])

    mine = {hops: along_x(hops) for hops in (2, 1, 3)}

    step = 3
    residual = call(
        functools.partial(residual_kernel, step),
        jax.ShapeDtypeStruct((SPAN, own_cols), F32),
        grid=(rows // step,),
        in_specs=[
            pl.BlockSpec((SPAN, step * QUAD), lambda i: (0, i)),
            pl.BlockSpec((SPAN, step * QUAD), lambda i: (0, i)),
            pl.BlockSpec((1, 16, LANES), lambda i: (0, 0, 0)),
            whole,
            whole,
        ],
        out_specs=pl.BlockSpec((SPAN, step * QUAD), lambda i: (0, i)),
        cost_estimate=pl.CostEstimate(flops=10**9, bytes_accessed=16 * 10**6, transcendentals=0),
    )(summed, m, own_ids, wide, ct)

    residual, mine[2] = lax.optimization_barrier((residual, mine[2]))
    beside, beside_far = across(field), across(mine[2])
    order = (1, 3)
    rest = jnp.stack([mine[hops] for hops in order])
    beside, beside_far, rest = lax.optimization_barrier((beside, beside_far, rest))
    x = lax.axis_index("x")

    def place(own, others, base):
        pieces = [*own.values(), *others.values()]
        last = () if base is None else (base,)
        return call(
            functools.partial(place_kernel, list(own), list(others)),
            jax.ShapeDtypeStruct((SPAN, columns), BF16),
            in_specs=[scalar] * 2 + [anywhere] * (len(pieces) + len(last)),
            out_specs=hbm,
            scratch_shapes=[dma((NX * NC * leaves,))],
            input_output_aliases={} if base is None else {len(pieces) + 2: 0},
            cost_estimate=pl.CostEstimate(flops=0, bytes_accessed=4 * 10**6, transcendentals=0),
        )(x.reshape(1), core.reshape(1), *pieces, *last)

    update = place({0: field, 2: mine[2], order: rest}, {0: beside, 2: beside_far}, None)
    update = place({}, {order: across(rest)}, update)
    return (residual[None], update)


def solution(mesh):
    reps, leaves = mesh.devices.shape
    nz = reps // (NX * NC)
    fine = Mesh(mesh.devices.reshape(NX, nz, NC, leaves), ("x", "z", "core", "leaf"))
    rep = ("x", "z", "core")
    placed = (
        P(rep, "leaf", None, None),
        P(rep, None, "leaf"),
        P(rep, None, "leaf", None),
        P(rep, None, "leaf"),
    )
    return jax.shard_map(
        functools.partial(on_device, nz, leaves),
        mesh=fine,
        in_specs=placed,
        out_specs=(P(rep, None, "leaf"), P()),
        check_vma=False,
    )
```

```python
import functools

import jax
import jax.numpy as jnp
import numpy as np
from jax import lax
from jax.experimental import pallas as pl
from jax.experimental.pallas import tpu as pltpu
from jax.sharding import Mesh, PartitionSpec as P

SPAN = 64
LANES = 128
QUAD = 4 * SPAN
NX, NC = 4, 2
F32, BF16 = jnp.float32, jnp.bfloat16
VMEM_LIMIT = 24 * 1024 * 1024


def split(a):
    hi = a.astype(BF16)
    return hi, (a - hi.astype(F32)).astype(BF16)


def tables():
    f = np.arange(SPAN)[:, None]
    i = np.arange(SPAN)[None, :]
    scale = np.where(f == 0, np.sqrt(1.0 / SPAN), np.sqrt(2.0 / SPAN))
    c = (scale * np.cos(np.pi * (2 * i + 1) * f / (2 * SPAN))).astype(np.float32)
    return c


def two_parts(c):
    hi = c.astype(jnp.bfloat16)
    lo = (c - hi.astype(np.float32)).astype(jnp.bfloat16)
    return hi, lo


def dot(a, b):
    return lax.dot_general(a, b, (((1,), (0,)), ((), ())), preferred_element_type=F32)


def dot_t(a, b):
    return lax.dot_general(a, b, (((1,), (1,)), ((), ())), preferred_element_type=F32)


def quads(x):
    n = x.shape[1] // QUAD
    return jnp.concatenate([x[:, QUAD * a : QUAD * (a + 1)] for a in range(n)], axis=0)


def lane_iota(shape):
    return lax.broadcasted_iota(jnp.int32, shape, len(shape) - 1)


def column_transform(x32, wide, hi_only):
    hi, lo = split(x32)
    both = dot(hi, wide)
    return both[:, :QUAD] + both[:, QUAD:] + dot(lo, hi_only)


def frequencies(ids):
    known = jnp.maximum(ids, 0)
    return lax.shift_right_logical(known, 6), jnp.bitwise_and(known, SPAN - 1)


def picked(f, ids, rows):
    lane = lane_iota((SPAN, LANES))
    _, v = frequencies(ids)
    at = jnp.broadcast_to(v, (SPAN, LANES)) + jnp.bitwise_and(lax.shift_left(lane, 1), SPAN)
    left = jnp.take_along_axis(f[:, :LANES], at, axis=1, mode="promise_in_bounds")
    right = jnp.take_along_axis(f[:, LANES:], at, axis=1, mode="promise_in_bounds")
    value = jnp.sum(jnp.where(lane < SPAN, left, right) * rows, axis=0, keepdims=True)
    return jnp.where(ids >= 0, value, 0.0)


def fetch(pairs, sems):
    copies = [pltpu.make_async_copy(src, dst, sems.at[i]) for i, (src, dst) in enumerate(pairs)]
    for copy in copies:
        copy.start()
    return copies


def ids_kernel(picks_hbm, counts_hbm, out_ref, picks_ref, counts_ref, sems):
    for copy in fetch([(picks_hbm, picks_ref), (counts_hbm, counts_ref)], sems):
        copy.wait()
    slots, n = picks_ref.shape
    slot = lax.broadcasted_iota(jnp.int32, (slots, n), 0)
    ids = jnp.where(slot < counts_ref[...], picks_ref[...], -1).T
    rows = n // 4
    lines = [
        jnp.concatenate([ids[4 * a + g : 4 * a + g + 1, :] for g in range(4)], axis=1)
        for a in range(rows)
    ]
    lines.append(jnp.full((out_ref.shape[1] - rows, LANES), -1, jnp.int32))
    full = jnp.concatenate(lines, axis=0)
    for y in range(out_ref.shape[0]):
        out_ref[y] = full


def dense_kernel(
    leaves, me_ref, g_hbm, m_hbm, wide_hbm, f_hbm, buf, m_ref, wide_ref, f_ref, sems, outs
):
    cols = g_hbm.shape[1] // leaves
    pairs = [(wide_hbm, wide_ref)]
    pairs += [(g_hbm.at[:, y * cols : (y + 1) * cols], buf.at[y]) for y in range(leaves)]
    pairs += [(m_hbm, m_ref)]
    copies = fetch(pairs, sems)
    copies[0].wait()
    me = me_ref[0]
    back = []
    for y in range(leaves):
        copies[1 + y].wait()
        both = dot(quads(buf[y]), wide_ref[...])
        f_ref[y] = both[:, :QUAD] + both[:, QUAD:]
        if y == 0:
            copies[leaves + 1].wait()

        @pl.when(me == y)
        def _():
            own = column_transform(quads(0.9 * m_ref[...]), wide_ref[...], wide_ref[:, :QUAD])
            f_ref[y] += own

        copy = pltpu.make_async_copy(f_ref.at[y], f_hbm.at[y], outs.at[y])
        copy.start()
        back.append(copy)
    for copy in back:
        copy.wait()


def coeff_kernel(rows, f_hbm, ids_hbm, tab_hbm, out_ref, f_ref, ids_ref, tab_ref, sems):
    leaves = f_hbm.shape[0]
    pairs = [(ids_hbm, ids_ref), (tab_hbm, tab_ref)]
    first, second, *copies = fetch(pairs + [(f_hbm.at[y], f_ref.at[y]) for y in range(leaves)], sems)
    first.wait()
    second.wait()
    both = jnp.concatenate([tab_ref[2], tab_ref[3]], axis=0)
    short = lax.broadcasted_iota(jnp.int32, (SPAN, LANES), 0)
    for y in range(leaves):
        lines = [ids_ref[y, a : a + 1, :] for a in range(rows)]
        hot = [jnp.where(short == frequencies(ids)[0], 1.0, 0.0).astype(BF16) for ids in lines]
        table = dot(both, jnp.concatenate(hot, axis=1))
        table = table[:SPAN] + table[SPAN:]
        copies[y].wait()
        for a in range(rows):
            f = f_ref[y, SPAN * a : SPAN * (a + 1), :]
            out_ref[y, a : a + 1, :] = picked(f, lines[a], table[:, LANES * a : LANES * (a + 1)])
        out_ref[y, rows:, :] = jnp.zeros((out_ref.shape[1] - rows, LANES), F32)


def regroup_kernel(per, got_ref, ids_ref, out_ref):
    total = got_ref[0]
    for l in range(1, got_ref.shape[0]):
        total = total + got_ref[l]
    total = total.astype(BF16).astype(F32)
    ids = jnp.maximum(ids_ref[0], 0).astype(F32)
    low = lane_iota((1, LANES)) < SPAN
    for x in range(NX):
        for c in range(NC):
            keep = low if c == 0 else jnp.logical_not(low)
            full, half = per * x + (per - 1) * c, per * x + 1
            value, index = total[half : half + 1], ids[half : half + 1]
            mixed = jnp.where(keep, value, pltpu.roll(index, SPAN, 1))
            page = jnp.concatenate([total[full : full + 1], mixed, ids[full : full + 1]], axis=1)
            for z in range(out_ref.shape[1]):
                out_ref[x, z, c] = page


def update_kernel(per, core_ref, got_ref, tab_hbm, out_ref, tab_ref, sems):
    (copy,) = fetch([(tab_hbm, tab_ref)], sems)
    peers = got_ref.shape[0]
    tall = lax.broadcasted_iota(jnp.int32, (2 * SPAN, LANES), 0)
    short = lax.broadcasted_iota(jnp.int32, (SPAN, LANES), 0)
    block = lax.shift_left(jnp.bitwise_and(lax.shift_right_logical(lane_iota((1, LANES)), 5), 1), 6)
    low = lane_iota((1, LANES)) < SPAN
    first_core = core_ref[0] == 0

    def two_peers(n):
        a, b = got_ref[n], got_ref[n + 1]
        mixed_a, mixed_b = a[:, LANES : 2 * LANES], b[:, LANES : 2 * LANES]
        turned_a, turned_b = pltpu.roll(mixed_a, SPAN, 1), pltpu.roll(mixed_b, SPAN, 1)
        firsts, seconds = [], []
        for at in (0, 2 * LANES):
            one, two = a[:, at : at + LANES], b[:, at : at + LANES]
            firsts.append(jnp.where(low, one, pltpu.roll(two, SPAN, 1)))
            seconds.append(jnp.where(low, pltpu.roll(one, SPAN, 1), two))
        here = jnp.where(low, mixed_a, turned_b)
        there = jnp.where(low, turned_a, mixed_b)
        value = jnp.where(first_core, here, there)
        index = jnp.where(first_core, there, here)
        return firsts, seconds, (value, index)

    def four_peers(n, sums):
        pairs = [two_peers(4 * n), two_peers(4 * n + 2)]
        new = []
        for a in range(per):
            left, right = [], []
            for lines in pairs:
                value, ids = lines[a][0], lines[a][1].astype(jnp.int32)
                u = lax.shift_right_logical(ids, 6) + block
                v = jnp.bitwise_and(ids, SPAN - 1)
                left.append(jnp.where(tall == u, value, 0.0).astype(BF16))
                right.append(jnp.where(short == v, 1.0, 0.0).astype(BF16))
            new.append(
                sums[a] + dot_t(jnp.concatenate(left, axis=1), jnp.concatenate(right, axis=1))
            )
        return tuple(new)

    zero = jnp.zeros((2 * SPAN, SPAN), F32)
    sums = lax.fori_loop(0, peers // 4, four_peers, (zero,) * per, unroll=True)
    z = jnp.concatenate(sums, axis=0)
    z_hi, z_lo = split(z)
    copy.wait()
    c_hi, c_lo, ct_hi, ct_lo = [tab_ref[i] for i in range(4)]
    w = dot(z_hi, c_hi) + (dot(z_hi, c_lo) + dot(z_lo, c_hi))
    flat = jnp.concatenate([w[SPAN * b : SPAN * (b + 1)] for b in range(2 * per)], axis=1)
    w_hi, w_lo = split(flat)
    field = dot(ct_hi, w_hi) + (dot(ct_lo, w_hi) + dot(ct_hi, w_lo))
    edge = 2 * LANES
    turned = jnp.concatenate([field[:, edge:], field[:, :edge]], axis=1)
    field = jnp.where(core_ref[0] == 0, field, turned).astype(BF16)
    for y in range(out_ref.shape[0]):
        out_ref[y] = field


def residual_kernel(step, sum_ref, m_ref, ids_ref, wide_ref, ct_ref, out_ref):
    first = pl.program_id(0) * step
    x = 0.9 * m_ref[...] + sum_ref[...].astype(F32)
    f = column_transform(quads(x), wide_ref[...], wide_ref[:, :QUAD])
    ct = ct_ref[...]
    group = lax.shift_right_logical(lane_iota((SPAN, LANES)), 5)
    for a in range(step):
        ids = ids_ref[0, pl.ds(first + a, 1), :]
        u, v = [jnp.broadcast_to(w, (SPAN, LANES)) for w in frequencies(ids)]
        rows = jnp.take_along_axis(ct, u, axis=1, mode="promise_in_bounds")
        cols = jnp.take_along_axis(ct, v, axis=1, mode="promise_in_bounds")
        value = picked(f[SPAN * a : SPAN * (a + 1)], ids, rows)
        cols = jnp.concatenate([jnp.where(group == b, cols, 0.0) for b in range(4)], axis=0)
        l_hi, l_lo = split(rows * value)
        r_hi, r_lo = split(cols)
        taken = dot_t(l_hi, r_hi) + (dot_t(l_hi, r_lo) + dot_t(l_lo, r_hi))
        out_ref[:, QUAD * a : QUAD * (a + 1)] = x[:, QUAD * a : QUAD * (a + 1)] - taken


def place_kernel(own, others, x_ref, core_ref, *refs):
    out_hbm, sem = refs[-2], refs[-1]
    x, core = x_ref[0], core_ref[0]
    pieces, at = [], []
    for hops, c, ref in zip(own + others, [core] * len(own) + [1 - core] * len(others), refs):
        several = hops if isinstance(hops, tuple) else (hops,)
        pieces += [ref.at[i] for i in range(len(several))] if hops is several else [ref]
        at += [jnp.bitwise_and(x + (NX - n), NX - 1) * NC + c for n in several]
    leaves, _, cols = pieces[0].shape
    copies = []
    for i, piece in enumerate(pieces):
        for y in range(leaves):
            to = pl.multiple_of((y * NX * NC + at[i]) * cols, LANES)
            copies.append(
                pltpu.make_async_copy(piece.at[y], out_hbm.at[:, pl.ds(to, cols)], sem.at[len(copies)])
            )
    for copy in copies:
        copy.start()
    for copy in copies:
        copy.wait()


def call(kernel, out_shape, vmem=VMEM_LIMIT, **kw):
    return pl.pallas_call(
        kernel,
        out_shape=out_shape,
        compiler_params=pltpu.CompilerParams(vmem_limit_bytes=vmem),
        **kw,
    )


def on_device(nz, leaves, grads, momentum, picks, counts):
    c = tables()
    c_hi, c_lo = two_parts(c)
    ct_hi, ct_lo = two_parts(np.ascontiguousarray(c.T))
    eye = np.eye(4, dtype=np.float32)
    bd_hi = np.kron(eye, ct_hi.astype(np.float32)).astype(jnp.bfloat16)
    bd_lo = np.kron(eye, ct_lo.astype(np.float32)).astype(jnp.bfloat16)
    wide = jnp.asarray(np.concatenate([bd_hi, bd_lo], axis=1))
    tab = jnp.asarray(np.stack([c_hi, c_lo, ct_hi, ct_lo]))
    ct = jnp.asarray(np.concatenate([c.T, c.T], axis=1))

    columns = grads.shape[3]
    own_cols = columns // leaves
    blocks, slots = picks.shape[2:]
    rows = blocks // 4
    per = rows // NX
    peers = nz * NC
    g = grads.reshape(SPAN, columns)
    m = momentum.reshape(SPAN, own_cols)
    leaf = lax.axis_index("leaf")
    core = lax.axis_index("core")
    whole = pl.BlockSpec(memory_space=pltpu.VMEM)
    scalar = pl.BlockSpec(memory_space=pltpu.SMEM)
    hbm = pl.BlockSpec(memory_space=pltpu.HBM)
    anywhere = pl.BlockSpec(memory_space=pl.ANY)
    dma = pltpu.SemaphoreType.DMA

    summed = lax.psum_scatter(g, "leaf", scatter_dimension=1, tiled=True)

    own_ids = call(
        ids_kernel,
        jax.ShapeDtypeStruct((leaves, 16, LANES), jnp.int32),
        vmem=62 * 1024 * 1024,
        in_specs=[hbm, hbm],
        scratch_shapes=[
            pltpu.VMEM((slots, blocks), jnp.int32),
            pltpu.VMEM((1, blocks), jnp.int32),
            dma((2,)),
        ],
    )(picks.reshape(blocks, slots).T, counts.reshape(1, blocks))
    all_ids = lax.all_to_all(own_ids, "leaf", 0, 0, tiled=True)

    f = call(
        functools.partial(dense_kernel, leaves),
        jax.ShapeDtypeStruct((leaves, rows * SPAN, QUAD), F32),
        vmem=56 * 1024 * 1024,
        in_specs=[scalar, hbm, hbm, hbm],
        out_specs=hbm,
        scratch_shapes=[
            pltpu.VMEM((leaves, SPAN, own_cols), BF16),
            pltpu.VMEM((SPAN, own_cols), F32),
            pltpu.VMEM(wide.shape, BF16),
            pltpu.VMEM((leaves, rows * SPAN, QUAD), F32),
            dma((leaves + 2,)),
            dma((leaves,)),
        ],
        cost_estimate=pl.CostEstimate(flops=2 * 10**9, bytes_accessed=16 * 10**6, transcendentals=0),
    )(leaf.reshape(1), g, m, wide)

    partial = call(
        functools.partial(coeff_kernel, rows),
        jax.ShapeDtypeStruct((leaves, 16, LANES), F32),
        vmem=50 * 1024 * 1024,
        in_specs=[hbm, anywhere, hbm],
        scratch_shapes=[
            pltpu.VMEM((leaves, rows * SPAN, QUAD), F32),
            pltpu.VMEM(all_ids.shape, jnp.int32),
            pltpu.VMEM(tab.shape, BF16),
            dma((leaves + 2,)),
        ],
    )(f, all_ids, tab)
    got = lax.all_to_all(partial, "leaf", 0, 0, tiled=True)

    sent = call(
        functools.partial(regroup_kernel, per),
        jax.ShapeDtypeStruct((NX, nz, NC, 1, 3 * LANES), F32),
    )(got, own_ids)
    got = lax.all_to_all(
        sent.reshape(NX * peers, 1, 3 * LANES), ("x", "z", "core"), 0, 0, tiled=True
    )

    wide_cols = 2 * per * SPAN
    field = call(
        functools.partial(update_kernel, per),
        jax.ShapeDtypeStruct((leaves, SPAN, wide_cols), BF16),
        in_specs=[scalar, whole, hbm],
        scratch_shapes=[pltpu.VMEM(tab.shape, BF16), dma((1,))],
    )(core.reshape(1), got, tab)
    summed, field = lax.optimization_barrier((summed, field))
    field = lax.all_to_all(field, "leaf", 0, 0, tiled=True)

    def along_x(hops):
        return lax.ppermute(field, "x", [(i, (i + hops) % NX) for i in range(NX)])

    def across(a):
        return lax.ppermute(a, "core", [(0, 1), (1, 0)])

    mine = {hops: along_x(hops) for hops in (2, 1, 3)}

    step = 3
    residual = call(
        functools.partial(residual_kernel, step),
        jax.ShapeDtypeStruct((SPAN, own_cols), F32),
        vmem=57 * 1024 * 1024,
        grid=(rows // step,),
        in_specs=[
            pl.BlockSpec((SPAN, step * QUAD), lambda i: (0, i)),
            pl.BlockSpec((SPAN, step * QUAD), lambda i: (0, i)),
            pl.BlockSpec((1, 16, LANES), lambda i: (0, 0, 0)),
            whole,
            whole,
        ],
        out_specs=pl.BlockSpec((SPAN, step * QUAD), lambda i: (0, i)),
        cost_estimate=pl.CostEstimate(flops=10**9, bytes_accessed=16 * 10**6, transcendentals=0),
    )(summed, m, own_ids, wide, ct)

    residual, mine[2] = lax.optimization_barrier((residual, mine[2]))
    beside, beside_far = across(field), across(mine[2])
    order = (1, 3)
    rest = jnp.stack([mine[hops] for hops in order])
    beside, beside_far, rest = lax.optimization_barrier((beside, beside_far, rest))
    x = lax.axis_index("x")

    def place(own, others, base):
        pieces = [*own.values(), *others.values()]
        last = () if base is None else (base,)
        return call(
            functools.partial(place_kernel, list(own), list(others)),
            jax.ShapeDtypeStruct((SPAN, columns), BF16),
            in_specs=[scalar] * 2 + [anywhere] * (len(pieces) + len(last)),
            out_specs=hbm,
            scratch_shapes=[dma((NX * NC * leaves,))],
            input_output_aliases={} if base is None else {len(pieces) + 2: 0},
            cost_estimate=pl.CostEstimate(flops=0, bytes_accessed=4 * 10**6, transcendentals=0),
        )(x.reshape(1), core.reshape(1), *pieces, *last)

    update = place({0: field, 2: mine[2], order: rest}, {0: beside, 2: beside_far}, None)
    update = place({}, {order: across(rest)}, update)
    return (residual[None], update)


def solution(mesh):
    reps, leaves = mesh.devices.shape
    nz = reps // (NX * NC)
    fine = Mesh(mesh.devices.reshape(NX, nz, NC, leaves), ("x", "z", "core", "leaf"))
    rep = ("x", "z", "core")
    placed = (
        P(rep, "leaf", None, None),
        P(rep, None, "leaf"),
        P(rep, None, "leaf", None),
        P(rep, None, "leaf"),
    )
    return jax.shard_map(
        functools.partial(on_device, nz, leaves),
        mesh=fine,
        in_specs=placed,
        out_specs=(P(rep, None, "leaf"), P()),
        check_vma=False,
    )
```

```python
import functools

import jax
import jax.numpy as jnp
import numpy as np
from jax import lax
from jax.experimental import pallas as pl
from jax.experimental.pallas import tpu as pltpu
from jax.sharding import Mesh, PartitionSpec as P

SPAN = 64
LANES = 128
QUAD = 4 * SPAN
NX, NC = 4, 2
F32, BF16 = jnp.float32, jnp.bfloat16
VMEM_LIMIT = 24 * 1024 * 1024


def split(a):
    hi = a.astype(BF16)
    return hi, (a - hi.astype(F32)).astype(BF16)


def tables():
    f = np.arange(SPAN)[:, None]
    i = np.arange(SPAN)[None, :]
    scale = np.where(f == 0, np.sqrt(1.0 / SPAN), np.sqrt(2.0 / SPAN))
    c = (scale * np.cos(np.pi * (2 * i + 1) * f / (2 * SPAN))).astype(np.float32)
    return c


def two_parts(c):
    hi = c.astype(jnp.bfloat16)
    lo = (c - hi.astype(np.float32)).astype(jnp.bfloat16)
    return hi, lo


def dot(a, b):
    return lax.dot_general(a, b, (((1,), (0,)), ((), ())), preferred_element_type=F32)


def dot_t(a, b):
    return lax.dot_general(a, b, (((1,), (1,)), ((), ())), preferred_element_type=F32)


def quads(x):
    n = x.shape[1] // QUAD
    return jnp.concatenate([x[:, QUAD * a : QUAD * (a + 1)] for a in range(n)], axis=0)


def lane_iota(shape):
    return lax.broadcasted_iota(jnp.int32, shape, len(shape) - 1)


def column_transform(x32, deep):
    hi, lo = split(x32)
    return dot(jnp.concatenate([hi, hi, lo], axis=1), deep)


def frequencies(ids):
    known = jnp.maximum(ids, 0)
    return lax.shift_right_logical(known, 6), jnp.bitwise_and(known, SPAN - 1)


def picked(f, ids, rows):
    lane = lane_iota((SPAN, LANES))
    _, v = frequencies(ids)
    at = jnp.broadcast_to(v, (SPAN, LANES)) + jnp.bitwise_and(lax.shift_left(lane, 1), SPAN)
    left = jnp.take_along_axis(f[:, :LANES], at, axis=1, mode="promise_in_bounds")
    right = jnp.take_along_axis(f[:, LANES:], at, axis=1, mode="promise_in_bounds")
    value = jnp.sum(jnp.where(lane < SPAN, left, right) * rows, axis=0, keepdims=True)
    return jnp.where(ids >= 0, value, 0.0)


def fetch(pairs, sems):
    copies = [pltpu.make_async_copy(src, dst, sems.at[i]) for i, (src, dst) in enumerate(pairs)]
    for copy in copies:
        copy.start()
    return copies


def ids_kernel(picks_hbm, counts_hbm, out_ref, picks_ref, counts_ref, sems):
    for copy in fetch([(picks_hbm, picks_ref), (counts_hbm, counts_ref)], sems):
        copy.wait()
    slots, n = picks_ref.shape
    slot = lax.broadcasted_iota(jnp.int32, (slots, n), 0)
    ids = jnp.where(slot < counts_ref[...], picks_ref[...], -1).T
    rows = n // 4
    lines = [
        jnp.concatenate([ids[4 * a + g : 4 * a + g + 1, :] for g in range(4)], axis=1)
        for a in range(rows)
    ]
    lines.append(jnp.full((out_ref.shape[1] - rows, LANES), -1, jnp.int32))
    full = jnp.concatenate(lines, axis=0)
    for y in range(out_ref.shape[0]):
        out_ref[y] = full


def dense_kernel(
    leaves, me_ref, g_hbm, m_hbm, wide_hbm, f_hbm, buf, m_ref, wide_ref, f_ref, sems, outs
):
    cols = g_hbm.shape[1] // leaves
    pairs = [(wide_hbm, wide_ref)]
    pairs += [(g_hbm.at[:, y * cols : (y + 1) * cols], buf.at[y]) for y in range(leaves)]
    pairs += [(m_hbm, m_ref)]
    copies = fetch(pairs, sems)
    copies[0].wait()
    me = me_ref[0]
    back = []
    for y in range(leaves):
        copies[1 + y].wait()
        x = quads(buf[y])
        f_ref[y] = dot(jnp.concatenate([x, x], axis=1), wide_ref[: 2 * QUAD, :])
        if y == 0:
            copies[leaves + 1].wait()

        @pl.when(me == y)
        def _():
            own = column_transform(quads(0.9 * m_ref[...]), wide_ref[...])
            f_ref[y] += own

        copy = pltpu.make_async_copy(f_ref.at[y], f_hbm.at[y], outs.at[y])
        copy.start()
        back.append(copy)
    for copy in back:
        copy.wait()


def coeff_kernel(rows, f_hbm, ids_hbm, tab_hbm, out_ref, f_ref, ids_ref, tab_ref, sems):
    leaves = f_hbm.shape[0]
    pairs = [(ids_hbm, ids_ref), (tab_hbm, tab_ref)]
    first, second, *copies = fetch(pairs + [(f_hbm.at[y], f_ref.at[y]) for y in range(leaves)], sems)
    first.wait()
    second.wait()
    both = jnp.concatenate([tab_ref[2], tab_ref[3]], axis=0)
    short = lax.broadcasted_iota(jnp.int32, (SPAN, LANES), 0)
    for y in range(leaves):
        lines = [ids_ref[y, a : a + 1, :] for a in range(rows)]
        hot = [jnp.where(short == frequencies(ids)[0], 1.0, 0.0).astype(BF16) for ids in lines]
        table = dot(both, jnp.concatenate(hot, axis=1))
        table = table[:SPAN] + table[SPAN:]
        copies[y].wait()
        for a in range(rows):
            f = f_ref[y, SPAN * a : SPAN * (a + 1), :]
            out_ref[y, a : a + 1, :] = picked(f, lines[a], table[:, LANES * a : LANES * (a + 1)])
        out_ref[y, rows:, :] = jnp.zeros((out_ref.shape[1] - rows, LANES), F32)


def regroup_kernel(per, got_ref, ids_ref, out_ref):
    total = got_ref[0]
    for l in range(1, got_ref.shape[0]):
        total = total + got_ref[l]
    total = total.astype(BF16).astype(F32)
    ids = jnp.maximum(ids_ref[0], 0).astype(F32)
    low = lane_iota((1, LANES)) < SPAN
    for x in range(NX):
        for c in range(NC):
            keep = low if c == 0 else jnp.logical_not(low)
            full, half = per * x + (per - 1) * c, per * x + 1
            value, index = total[half : half + 1], ids[half : half + 1]
            mixed = jnp.where(keep, value, pltpu.roll(index, SPAN, 1))
            page = jnp.concatenate([total[full : full + 1], mixed, ids[full : full + 1]], axis=1)
            for z in range(out_ref.shape[1]):
                out_ref[x, z, c] = page


def update_kernel(per, core_ref, got_ref, tab_hbm, out_ref, tab_ref, sems):
    (copy,) = fetch([(tab_hbm, tab_ref)], sems)
    peers = got_ref.shape[0]
    tall = lax.broadcasted_iota(jnp.int32, (2 * SPAN, LANES), 0)
    short = lax.broadcasted_iota(jnp.int32, (SPAN, LANES), 0)
    block = lax.shift_left(jnp.bitwise_and(lax.shift_right_logical(lane_iota((1, LANES)), 5), 1), 6)
    low = lane_iota((1, LANES)) < SPAN
    first_core = core_ref[0] == 0

    def two_peers(n):
        a, b = got_ref[n], got_ref[n + 1]
        mixed_a, mixed_b = a[:, LANES : 2 * LANES], b[:, LANES : 2 * LANES]
        turned_a, turned_b = pltpu.roll(mixed_a, SPAN, 1), pltpu.roll(mixed_b, SPAN, 1)
        firsts, seconds = [], []
        for at in (0, 2 * LANES):
            one, two = a[:, at : at + LANES], b[:, at : at + LANES]
            firsts.append(jnp.where(low, one, pltpu.roll(two, SPAN, 1)))
            seconds.append(jnp.where(low, pltpu.roll(one, SPAN, 1), two))
        here = jnp.where(low, mixed_a, turned_b)
        there = jnp.where(low, turned_a, mixed_b)
        value = jnp.where(first_core, here, there)
        index = jnp.where(first_core, there, here)
        return firsts, seconds, (value, index)

    def four_peers(n, sums):
        pairs = [two_peers(4 * n), two_peers(4 * n + 2)]
        new = []
        for a in range(per):
            left, right = [], []
            for lines in pairs:
                value, ids = lines[a][0], lines[a][1].astype(jnp.int32)
                u = lax.shift_right_logical(ids, 6) + block
                v = jnp.bitwise_and(ids, SPAN - 1)
                left.append(jnp.where(tall == u, value, 0.0).astype(BF16))
                right.append(jnp.where(short == v, 1.0, 0.0).astype(BF16))
            new.append(
                sums[a] + dot_t(jnp.concatenate(left, axis=1), jnp.concatenate(right, axis=1))
            )
        return tuple(new)

    zero = jnp.zeros((2 * SPAN, SPAN), F32)
    sums = lax.fori_loop(0, peers // 4, four_peers, (zero,) * per, unroll=True)
    z = jnp.concatenate(sums, axis=0)
    z_hi, z_lo = split(z)
    copy.wait()
    c_hi, c_lo, ct_hi, ct_lo = [tab_ref[i] for i in range(4)]
    w = dot(z_hi, c_hi) + (dot(z_hi, c_lo) + dot(z_lo, c_hi))
    flat = jnp.concatenate([w[SPAN * b : SPAN * (b + 1)] for b in range(2 * per)], axis=1)
    w_hi, w_lo = split(flat)
    field = dot(ct_hi, w_hi) + (dot(ct_lo, w_hi) + dot(ct_hi, w_lo))
    edge = 2 * LANES
    turned = jnp.concatenate([field[:, edge:], field[:, :edge]], axis=1)
    field = jnp.where(core_ref[0] == 0, field, turned).astype(BF16)
    for y in range(out_ref.shape[0]):
        out_ref[y] = field


def residual_kernel(step, sum_ref, m_ref, ids_ref, wide_ref, ct_ref, out_ref):
    first = pl.program_id(0) * step
    x = 0.9 * m_ref[...] + sum_ref[...].astype(F32)
    f = column_transform(quads(x), wide_ref[...])
    ct = ct_ref[...]
    group = lax.shift_right_logical(lane_iota((SPAN, LANES)), 5)
    for a in range(step):
        ids = ids_ref[0, pl.ds(first + a, 1), :]
        u, v = [jnp.broadcast_to(w, (SPAN, LANES)) for w in frequencies(ids)]
        rows = jnp.take_along_axis(ct, u, axis=1, mode="promise_in_bounds")
        cols = jnp.take_along_axis(ct, v, axis=1, mode="promise_in_bounds")
        value = picked(f[SPAN * a : SPAN * (a + 1)], ids, rows)
        cols = jnp.concatenate([jnp.where(group == b, cols, 0.0) for b in range(4)], axis=0)
        l_hi, l_lo = split(rows * value)
        r_hi, r_lo = split(cols)
        taken = dot_t(l_hi, r_hi) + (dot_t(l_hi, r_lo) + dot_t(l_lo, r_hi))
        out_ref[:, QUAD * a : QUAD * (a + 1)] = x[:, QUAD * a : QUAD * (a + 1)] - taken


def place_kernel(own, others, x_ref, core_ref, *refs):
    out_hbm, sem = refs[-2], refs[-1]
    x, core = x_ref[0], core_ref[0]
    pieces, at = [], []
    for hops, c, ref in zip(own + others, [core] * len(own) + [1 - core] * len(others), refs):
        several = hops if isinstance(hops, tuple) else (hops,)
        pieces += [ref.at[i] for i in range(len(several))] if hops is several else [ref]
        at += [jnp.bitwise_and(x + (NX - n), NX - 1) * NC + c for n in several]
    leaves, _, cols = pieces[0].shape
    copies = []
    for i, piece in enumerate(pieces):
        for y in range(leaves):
            to = pl.multiple_of((y * NX * NC + at[i]) * cols, LANES)
            copies.append(
                pltpu.make_async_copy(piece.at[y], out_hbm.at[:, pl.ds(to, cols)], sem.at[len(copies)])
            )
    for copy in copies:
        copy.start()
    for copy in copies:
        copy.wait()


def call(kernel, out_shape, vmem=VMEM_LIMIT, **kw):
    return pl.pallas_call(
        kernel,
        out_shape=out_shape,
        compiler_params=pltpu.CompilerParams(vmem_limit_bytes=vmem),
        **kw,
    )


def on_device(nz, leaves, grads, momentum, picks, counts):
    c = tables()
    c_hi, c_lo = two_parts(c)
    ct_hi, ct_lo = two_parts(np.ascontiguousarray(c.T))
    eye = np.eye(4, dtype=np.float32)
    bd_hi = np.kron(eye, ct_hi.astype(np.float32)).astype(jnp.bfloat16)
    bd_lo = np.kron(eye, ct_lo.astype(np.float32)).astype(jnp.bfloat16)
    wide = jnp.asarray(np.concatenate([bd_hi, bd_lo, bd_hi], axis=0))
    tab = jnp.asarray(np.stack([c_hi, c_lo, ct_hi, ct_lo]))
    ct = jnp.asarray(np.concatenate([c.T, c.T], axis=1))

    columns = grads.shape[3]
    own_cols = columns // leaves
    blocks, slots = picks.shape[2:]
    rows = blocks // 4
    per = rows // NX
    peers = nz * NC
    g = grads.reshape(SPAN, columns)
    m = momentum.reshape(SPAN, own_cols)
    leaf = lax.axis_index("leaf")
    core = lax.axis_index("core")
    whole = pl.BlockSpec(memory_space=pltpu.VMEM)
    scalar = pl.BlockSpec(memory_space=pltpu.SMEM)
    hbm = pl.BlockSpec(memory_space=pltpu.HBM)
    anywhere = pl.BlockSpec(memory_space=pl.ANY)
    dma = pltpu.SemaphoreType.DMA

    summed = lax.psum_scatter(g, "leaf", scatter_dimension=1, tiled=True)

    own_ids = call(
        ids_kernel,
        jax.ShapeDtypeStruct((leaves, 16, LANES), jnp.int32),
        vmem=62 * 1024 * 1024,
        in_specs=[hbm, hbm],
        scratch_shapes=[
            pltpu.VMEM((slots, blocks), jnp.int32),
            pltpu.VMEM((1, blocks), jnp.int32),
            dma((2,)),
        ],
    )(picks.reshape(blocks, slots).T, counts.reshape(1, blocks))
    all_ids = lax.all_to_all(own_ids, "leaf", 0, 0, tiled=True)

    f = call(
        functools.partial(dense_kernel, leaves),
        jax.ShapeDtypeStruct((leaves, rows * SPAN, QUAD), F32),
        vmem=56 * 1024 * 1024,
        in_specs=[scalar, hbm, hbm, hbm],
        out_specs=hbm,
        scratch_shapes=[
            pltpu.VMEM((leaves, SPAN, own_cols), BF16),
            pltpu.VMEM((SPAN, own_cols), F32),
            pltpu.VMEM(wide.shape, BF16),
            pltpu.VMEM((leaves, rows * SPAN, QUAD), F32),
            dma((leaves + 2,)),
            dma((leaves,)),
        ],
        cost_estimate=pl.CostEstimate(flops=2 * 10**9, bytes_accessed=16 * 10**6, transcendentals=0),
    )(leaf.reshape(1), g, m, wide)

    partial = call(
        functools.partial(coeff_kernel, rows),
        jax.ShapeDtypeStruct((leaves, 16, LANES), F32),
        vmem=50 * 1024 * 1024,
        in_specs=[hbm, anywhere, hbm],
        scratch_shapes=[
            pltpu.VMEM((leaves, rows * SPAN, QUAD), F32),
            pltpu.VMEM(all_ids.shape, jnp.int32),
            pltpu.VMEM(tab.shape, BF16),
            dma((leaves + 2,)),
        ],
    )(f, all_ids, tab)
    got = lax.all_to_all(partial, "leaf", 0, 0, tiled=True)

    sent = call(
        functools.partial(regroup_kernel, per),
        jax.ShapeDtypeStruct((NX, nz, NC, 1, 3 * LANES), F32),
    )(got, own_ids)
    got = lax.all_to_all(
        sent.reshape(NX * peers, 1, 3 * LANES), ("x", "z", "core"), 0, 0, tiled=True
    )

    wide_cols = 2 * per * SPAN
    field = call(
        functools.partial(update_kernel, per),
        jax.ShapeDtypeStruct((leaves, SPAN, wide_cols), BF16),
        in_specs=[scalar, whole, hbm],
        scratch_shapes=[pltpu.VMEM(tab.shape, BF16), dma((1,))],
    )(core.reshape(1), got, tab)
    summed, field = lax.optimization_barrier((summed, field))
    field = lax.all_to_all(field, "leaf", 0, 0, tiled=True)

    def along_x(hops):
        return lax.ppermute(field, "x", [(i, (i + hops) % NX) for i in range(NX)])

    def across(a):
        return lax.ppermute(a, "core", [(0, 1), (1, 0)])

    mine = {hops: along_x(hops) for hops in (2, 1, 3)}

    step = 3
    residual = call(
        functools.partial(residual_kernel, step),
        jax.ShapeDtypeStruct((SPAN, own_cols), F32),
        vmem=57 * 1024 * 1024,
        grid=(rows // step,),
        in_specs=[
            pl.BlockSpec((SPAN, step * QUAD), lambda i: (0, i)),
            pl.BlockSpec((SPAN, step * QUAD), lambda i: (0, i)),
            pl.BlockSpec((1, 16, LANES), lambda i: (0, 0, 0)),
            whole,
            whole,
        ],
        out_specs=pl.BlockSpec((SPAN, step * QUAD), lambda i: (0, i)),
        cost_estimate=pl.CostEstimate(flops=10**9, bytes_accessed=16 * 10**6, transcendentals=0),
    )(summed, m, own_ids, wide, ct)

    residual, mine[2] = lax.optimization_barrier((residual, mine[2]))
    beside, beside_far = across(field), across(mine[2])
    order = (1, 3)
    rest = jnp.stack([mine[hops] for hops in order])
    beside, beside_far, rest = lax.optimization_barrier((beside, beside_far, rest))
    x = lax.axis_index("x")

    def place(own, others, base):
        pieces = [*own.values(), *others.values()]
        last = () if base is None else (base,)
        return call(
            functools.partial(place_kernel, list(own), list(others)),
            jax.ShapeDtypeStruct((SPAN, columns), BF16),
            in_specs=[scalar] * 2 + [anywhere] * (len(pieces) + len(last)),
            out_specs=hbm,
            scratch_shapes=[dma((NX * NC * leaves,))],
            input_output_aliases={} if base is None else {len(pieces) + 2: 0},
            cost_estimate=pl.CostEstimate(flops=0, bytes_accessed=4 * 10**6, transcendentals=0),
        )(x.reshape(1), core.reshape(1), *pieces, *last)

    update = place({0: field, 2: mine[2], order: rest}, {0: beside, 2: beside_far}, None)
    update = place({}, {order: across(rest)}, update)
    return (residual[None], update)


def solution(mesh):
    reps, leaves = mesh.devices.shape
    nz = reps // (NX * NC)
    fine = Mesh(mesh.devices.reshape(NX, nz, NC, leaves), ("x", "z", "core", "leaf"))
    rep = ("x", "z", "core")
    placed = (
        P(rep, "leaf", None, None),
        P(rep, None, "leaf"),
        P(rep, None, "leaf", None),
        P(rep, None, "leaf"),
    )
    return jax.shard_map(
        functools.partial(on_device, nz, leaves),
        mesh=fine,
        in_specs=placed,
        out_specs=(P(rep, None, "leaf"), P()),
        check_vma=False,
    )
```
